32 devices in a mesh: expert: 4 (over z), dp: 4 (over x, core), tensor: 2 (over y).
Axes of the slice: x: 2, y: 2, z: 4, core: 2. Of those that a mesh axis runs over, the one named last changes fastest.
Arguments:
- tokens: bfloat16 [2, 512, 7168], P(None, ('expert', 'dp')), may hold values from -6 to 6
- cotangent: bfloat16 [2, 512, 7168], P(None, ('expert', 'dp')), may hold values from -0.625 to 0.625
- route_gate: bfloat16 [2, 512, 2], P(None, ('expert', 'dp')), may hold values from 0.19921875 to 1
- routes: int32 [2, 512, 2], P(None, ('expert', 'dp')), may hold values from 0 to 3, all different within a row; in each aligned block of 32 rows (0 to 31, 32 to 63, ..., all dimensions but the last counted through in order) at most 24 rows name the same one
- gate_weight: bfloat16 [4, 7168, 1024], P('expert', 'dp', 'tensor'), may hold values from -0.0625 to 0.0625
- up_weight: bfloat16 [4, 7168, 1024], P('expert', 'dp', 'tensor'), may hold values from -0.0625 to 0.0625
- down_weight: bfloat16 [4, 1024, 7168], P('expert', 'tensor', 'dp'), may hold values from -0.1875 to 0.1875
- dropped: int32 [4, 3], P('expert'), may hold values from 0 to 7, as said below
Outputs:
- saliency: float32 [2, 4, 1024], P(None, 'expert', 'tensor')
- compact_down: bfloat16 [4, 640, 7168], P('expert', 'tensor', 'dp')
The draws below stay inside these ranges and needn't reach their ends.
Inputs may be any that keep to these rules, and one draw needn't show every extreme that they name: `routes`: each token names 2 different experts. Among the 32 tokens of one set on one index of expert and dp, no expert is named more than 24 times, a bound that some block reaches. `dropped`: each row lists 3 different block numbers.
All inputs are finite; a program needn't handle non-finite values.
Results may differ from the reference program's by a relative error of at most 0.001.
Values may be sent and summed in bfloat16 or wider, within the bound.
No kernel may reach another device: no remote copies, remote signals or barrier semaphores. Data moves between devices by JAX's collectives and lax.ppermute only.
A program may use at most 128 MiB of HBM per device.

```python
import math
import jax
import jax.numpy as jnp
import numpy as np
from jax import lax

D = 7168
FF = 1024
TOP = 2
TOK_DEV = 32
BLOCK = 128
DROP = 3
EXPERTS = 4
TOKENS = 512
CAP = 24
NBLK = 8
KEEP = 5


def draw_dropped(key, part):
    key_list = jax.random.split(key, EXPERTS)
    shuffled = jax.vmap(lambda single_key: jax.random.permutation(single_key, NBLK))(key_list)
    return shuffled[:, :DROP].astype(jnp.int32)


def levels(key, extent, cuts, least, high):
    def one(position, shards_of):
        steps = jax.random.uniform(jax.random.fold_in(jax.random.fold_in(key, 6), position), (shards_of,), jnp.float32, least / len(cuts), high / len(cuts))
        return jnp.repeat(jnp.exp(steps), extent[position] // shards_of).reshape((-1,) + (1,) * (len(extent) - position - 1))

    loudness = one(*cuts[0])
    for cut in cuts[1:]:
        loudness = loudness * one(*cut)
    return loudness


def assign_block(stream_key, own, number, rows, number_of, top, most, skew):
    order = jax.random.permutation(stream_key, number_of)
    crowded, usual = portions_of(number_of, rows * top, most, skew, True), portions_of(number_of, rows * top, most, skew, False)
    places = jnp.arange(number_of)

    def named(sizes, rotation):
        used = int((sizes > 0).sum())
        fixed = max(1, used // 4)
        moved = fixed + (places - fixed + rotation * (used - fixed)) % max(1, number_of - fixed)
        return jnp.zeros((number_of,), jnp.int32).at[order[jnp.where(places < fixed, places, moved)]].set(jnp.asarray(sizes, jnp.int32))

    sizes = jnp.where(number % 4 == 0, named(crowded, number // 4), named(usual, number - number // 4 - 1))
    mixed = jax.random.permutation(jax.random.fold_in(own, 3), number_of)
    source_of, taker = mixed[0:number_of // 2 * 2:2], mixed[1:number_of // 2 * 2:2]
    room = jnp.minimum(sizes[source_of] - 1, most - sizes[taker]) // 2
    room = jnp.where((source_of == order[0]) | (taker == order[0]) | (sizes[taker] == 0), 0, jnp.maximum(room, 0))
    moved = jax.random.randint(jax.random.fold_in(own, 4), (number_of // 2,), 0, 1 << 20) % (room + 1)
    sizes = sizes.at[source_of].add(-moved).at[taker].add(moved)
    labels = jnp.searchsorted(jnp.cumsum(sizes), jnp.arange(rows * top), side="right").astype(jnp.int32)
    listing = labels.reshape(top, rows).T
    listing = listing[jax.random.permutation(jax.random.fold_in(own, 1), rows)]
    rotation = jax.random.randint(jax.random.fold_in(own, 2), (rows, 1), 0, top)
    return jnp.take_along_axis(listing, (jnp.arange(top)[None, :] + rotation) % top, axis=1)


def portions_of(number_of, total, reach, skew, full):
    loads = [(1 << 20) // math.isqrt(standing ** skew) + 1 for standing in range(1, number_of + 1)]
    largest = reach if full else min(reach, max(-(-total // number_of), total * loads[0] // sum(loads)))
    least = 1 if total - largest >= number_of - 1 else 0
    counts, surplus = [largest] + [least] * (number_of - 1), total - largest - least * (number_of - 1)
    while surplus > 0:
        candidates = [i for i in range(1, number_of) if counts[i] < largest] or [i for i in range(1, number_of) if counts[i] < reach]
        pool, budget = sum([loads[i] for i in candidates]), surplus
        for i in candidates:
            addition = min(reach - counts[i], max(1, budget * loads[i] // pool), surplus)
            counts[i] = counts[i] + addition
            surplus = surplus - addition
    return np.array(counts)


def noise(key, shape, spread, most, cuts=(), held_as=jnp.bfloat16):
    result = spread * jax.random.normal(key, shape, jnp.float32)
    if cuts:
        result = result * levels(key, shape, cuts, -0.22, 0.18)
    return jnp.clip(result, -most, most).astype(held_as)


def setup_inputs(seed: int = 0) -> dict:
    arg_keys = jax.random.split(jax.random.key(seed), 9)
    tokens = noise(arg_keys[0], (2, TOKENS, D), 1.0, 6.0, ((1, 16),))
    cotangent = noise(arg_keys[1], (2, TOKENS, D), 0.1, 0.625, ((1, 16),))
    route_gate = jnp.clip(0.19921875 + 0.80078125 * jax.random.uniform(arg_keys[2], (2, TOKENS, TOP), jnp.float32) ** levels(arg_keys[2], (2, TOKENS, TOP), ((1, 16),), -0.2, 0.2), 0.19921875, 1.0).astype(jnp.bfloat16)
    routes_keys = jax.random.split(jax.random.fold_in(arg_keys[3], 1), 2 * TOKENS // TOK_DEV)
    routes_turns = jax.random.permutation(jax.random.fold_in(arg_keys[3], 3), 2 * TOKENS // TOK_DEV)
    routes = jax.vmap(lambda own, number: assign_block(jax.random.fold_in(arg_keys[3], 2), own, number, TOK_DEV, EXPERTS, TOP, CAP, 2))(routes_keys, routes_turns).reshape((2, TOKENS, TOP))
    gate_weight = noise(arg_keys[4], (EXPERTS, D, FF), D ** -0.5, 0.0625, ((0, 4), (1, 4), (2, 2)))
    up_weight = noise(arg_keys[5], (EXPERTS, D, FF), D ** -0.5, 0.0625, ((0, 4), (1, 4), (2, 2)))
    down_weight = noise(arg_keys[6], (EXPERTS, FF, D), FF ** -0.5, 0.1875, ((0, 4), (1, 2), (2, 4)))
    dropped = draw_dropped(jax.random.fold_in(arg_keys[8], 71), 0)
    return dict(tokens=tokens, cotangent=cotangent, route_gate=route_gate, routes=routes, gate_weight=gate_weight, up_weight=up_weight, down_weight=down_weight, dropped=dropped)


def reference(tokens, cotangent, route_gate, routes, gate_weight, up_weight, down_weight, dropped):
    most_rows = TOKENS // TOK_DEV * CAP

    def one_expert(expert_id):
        def one_set(set_index):
            matched = routes[set_index] == expert_id
            weight_sum = jnp.sum(jnp.where(matched, route_gate[set_index].astype(jnp.float32), 0.0), axis=1)
            used = jnp.any(matched, axis=1)
            picked = jnp.nonzero(used, size=most_rows, fill_value=0)[0].astype(jnp.int32)
            valid = jnp.arange(most_rows, dtype=jnp.int32) < jnp.sum(used.astype(jnp.int32))
            rows_in = tokens[set_index][picked]
            gate_act = jnp.dot(rows_in, gate_weight[expert_id], preferred_element_type=jnp.float32)
            up_act = jnp.dot(rows_in, up_weight[expert_id], preferred_element_type=jnp.float32)
            hidden = jax.nn.silu(gate_act) * up_act
            scaled = jnp.where(valid, weight_sum[picked], 0.0)
            product = jnp.dot(cotangent[set_index][picked], down_weight[expert_id].T, preferred_element_type=jnp.float32)
            hidden_grad = scaled[:, None] * product
            return jnp.abs(jnp.sum(hidden * hidden_grad, axis=0))

        return jnp.stack([one_set(0), one_set(1)])

    per_expert = lax.map(one_expert, jnp.arange(EXPERTS, dtype=jnp.int32))
    saliency = jnp.transpose(per_expert, (1, 0, 2))

    blocks = jnp.arange(NBLK, dtype=jnp.int32)
    kept_flag = jnp.all(dropped[:, :, None] != blocks[None, None, :], axis=1)
    ranking = jnp.cumsum(kept_flag.astype(jnp.int32), axis=1) - 1
    slots_kept = jnp.arange(KEEP, dtype=jnp.int32)
    selected = kept_flag[:, None, :] & (ranking[:, None, :] == slots_kept[None, :, None])
    source_block = jnp.sum(jnp.where(selected, blocks[None, None, :], 0), axis=2).astype(jnp.int32)
    grouped = down_weight.reshape(EXPERTS, NBLK, BLOCK, D)
    gathered = jax.vmap(lambda group_rows, choice_rows: group_rows[choice_rows])(grouped, source_block)
    compact_down = gathered.reshape(EXPERTS, KEEP * BLOCK, D)
    return saliency, compact_down
```

```python
import functools

import jax
import jax.numpy as jnp
from jax import lax
from jax.experimental import pallas as pl
from jax.experimental.pallas import tpu as pltpu
from jax.sharding import PartitionSpec as P

BLOCK = 128
NBLK = 8
KEEP = 5
LANES = 128
HALF = 64
MIB = 1 << 20


def capacity_of(tok_rows, top_count, experts):
    return min(tok_rows, max(2, 3 * tok_rows * top_count // (2 * experts)))


def neuron_terms(x_recv, grad_recv, gate_recv, gate_full, up_full, down_full):
    gate_act = jnp.einsum("pscd,df->pscf", x_recv, gate_full, preferred_element_type=jnp.float32)
    up_act = jnp.einsum("pscd,df->pscf", x_recv, up_full, preferred_element_type=jnp.float32)
    hidden = jax.nn.silu(gate_act) * up_act
    product = jnp.einsum("pscd,fd->pscf", grad_recv, down_full, preferred_element_type=jnp.float32)
    hidden_grad = gate_recv.astype(jnp.float32)[..., None] * product
    return jnp.sum(hidden * hidden_grad, axis=(0, 2))


def kept_blocks(dropped):
    blocks = jnp.arange(NBLK, dtype=jnp.int32)
    kept_flag = jnp.all(dropped[0][:, None] != blocks[None, :], axis=0)
    ranking = jnp.cumsum(kept_flag.astype(jnp.int32)) - 1
    ranks = jnp.arange(KEEP, dtype=jnp.int32)
    chosen = kept_flag[None, :] & (ranking[None, :] == ranks[:, None])
    return jnp.sum(jnp.where(chosen, blocks[None, :], 0), axis=1), kept_flag


def general_body(tokens, cotangent, route_gate, routes, gate_weight, up_weight, down_weight, dropped):
    experts = lax.axis_size("expert")
    tensor_count = lax.axis_size("tensor")
    tensor_pos = lax.axis_index("tensor")
    tok_rows = tokens.shape[1]
    capacity = capacity_of(tok_rows, routes.shape[2], experts)
    expert_ids = jnp.arange(experts, dtype=jnp.int32)
    matched = routes[:, :, :, None] == expert_ids
    chosen = jnp.any(matched, axis=2).astype(jnp.float32)
    weight_sum = jnp.sum(
        jnp.where(matched, route_gate.astype(jnp.float32)[:, :, :, None], 0.0), axis=2
    )
    earlier = jnp.cumsum(chosen, axis=1) - chosen
    placing = chosen[..., None] * (earlier[..., None] == jnp.arange(capacity, dtype=jnp.float32))
    slot_gate = jnp.einsum("stec,ste->esc", placing, weight_sum, precision=lax.Precision.HIGHEST)
    gate_slots = slot_gate.astype(jnp.bfloat16)
    placing_half = placing.astype(jnp.bfloat16)
    gate_full = lax.all_gather(gate_weight, "dp", axis=1, tiled=True)[0]
    up_full = lax.all_gather(up_weight, "dp", axis=1, tiled=True)[0]
    down_full = lax.all_gather(down_weight, "dp", axis=2, tiled=True)[0]
    x_slots = jnp.einsum(
        "stec,std->escd", placing_half, tokens, preferred_element_type=jnp.float32
    ).astype(jnp.bfloat16)
    grad_slots = jnp.einsum(
        "stec,std->escd", placing_half, cotangent, preferred_element_type=jnp.float32
    ).astype(jnp.bfloat16)
    partial_terms = neuron_terms(
        lax.all_to_all(x_slots, "expert", split_axis=0, concat_axis=0, tiled=True),
        lax.all_to_all(grad_slots, "expert", split_axis=0, concat_axis=0, tiled=True),
        lax.all_to_all(gate_slots, "expert", split_axis=0, concat_axis=0, tiled=True),
        gate_full,
        up_full,
        down_full,
    )
    totals = lax.psum(partial_terms, "dp")
    saliency = jnp.abs(totals)[:, None, :]
    rows_out = KEEP * BLOCK // tensor_count
    whole_rows = lax.all_gather(down_weight, "tensor", axis=1, tiled=True)[0]
    target_rows = tensor_pos * rows_out + jnp.arange(rows_out, dtype=jnp.int32)
    source_rows = kept_blocks(dropped)[0][target_rows // BLOCK] * BLOCK + target_rows % BLOCK
    compact_down = jnp.take(whole_rows, source_rows, axis=0)[None]
    return (saliency, compact_down)


def full(shape):
    return pl.BlockSpec(shape, lambda *_: (0,) * len(shape))


def pack_kernel(experts, cap, info, routes, gates, tokens, cotangent, *outs):
    messages, near, local, slot_gates = outs[:-3], outs[-3], outs[-2], outs[-1]
    z, x, core, y = info[0], info[1], info[2], info[3]
    rows = tokens.shape[1]
    chunk = near.shape[1] // 2
    lane = lax.broadcasted_iota(jnp.int32, (rows, LANES), 1)
    ahead = jnp.zeros_like(lane)
    for k in range(1, experts):
        ahead = ahead + (lane >= k * cap).astype(jnp.int32)
    slot = lane - ahead * cap
    expert = z + ahead
    expert = jnp.where(expert >= experts, expert - experts, expert)
    expert = jnp.where(lane < experts * cap, expert, -1)
    lower = (
        lax.broadcasted_iota(jnp.int32, (rows, rows), 1)
        < lax.broadcasted_iota(jnp.int32, (rows, rows), 0)
    ).astype(jnp.bfloat16)
    sets, placings, gate_rows = (y, 1 - y), [], []
    for s in sets:
        route, weight = routes[s], gates[s].astype(jnp.float32)
        match = jnp.zeros(lane.shape, jnp.float32)
        named = jnp.zeros(lane.shape, jnp.float32)
        for k in range(route.shape[1]):
            same = route[:, k : k + 1] == expert
            match = match + jnp.where(same, 1.0, 0.0)
            named = named + jnp.where(same, weight[:, k : k + 1], 0.0)
        rank = jnp.dot(lower, match.astype(jnp.bfloat16), preferred_element_type=jnp.float32)
        placing = jnp.where(rank == slot.astype(jnp.float32), match, 0.0)
        gate_rows.append(jnp.sum(placing * named, axis=0, keepdims=True))
        placings.append(placing.astype(jnp.bfloat16))
    slot_gates[...] = jnp.concatenate(
        gate_rows + [jnp.zeros((slot_gates.shape[0] - 2, LANES), jnp.float32)], axis=0
    )
    for dx in range(2):
        half = x if dx == 0 else 1 - x
        for h in range(2):
            column = pl.multiple_of((2 * half + (core if h == 0 else 1 - core)) * chunk, LANES)
            here = slice(h * chunk, (h + 1) * chunk)
            found = [
                lax.dot_general(
                    placing,
                    source[s, :, pl.ds(column, chunk)],
                    (((0,), (0,)), ((), ())),
                    preferred_element_type=jnp.float32,
                )
                for s, placing in zip(sets, placings)
                for source in (tokens, cotangent)
            ]
            for k in range(1, experts):
                span = slice(k * cap, (k + 1) * cap)
                messages[2 * (k - 1) + dx][:, here] = jnp.concatenate(
                    [found[0][span], found[1][span]], axis=0
                ).astype(jnp.bfloat16)
            (local if dx == 0 else near)[:, here] = jnp.concatenate(
                [part[:cap] for part in found], axis=0
            ).astype(jnp.bfloat16)


def pack(info, routes, gates, tokens, cotangent, experts, cap, width):
    one = jax.ShapeDtypeStruct((2 * cap, width), jnp.bfloat16)
    two = jax.ShapeDtypeStruct((4 * cap, width), jnp.bfloat16)
    outs = [one] * (2 * (experts - 1)) + [two, two, jax.ShapeDtypeStruct((8, LANES), jnp.float32)]
    return pl.pallas_call(
        functools.partial(pack_kernel, experts, cap),
        out_shape=outs,
        in_specs=[pl.BlockSpec(memory_space=pltpu.SMEM)] + [pl.BlockSpec(memory_space=pltpu.VMEM)] * 4,
        out_specs=[pl.BlockSpec(memory_space=pltpu.VMEM)] * len(outs),
        compiler_params=pltpu.CompilerParams(vmem_limit_bytes=32 * MIB),
        cost_estimate=pl.CostEstimate(flops=10**9, bytes_accessed=6 * 10**6, transcendentals=0),
        name="pack_rows",
    )(info, routes, gates, tokens, cotangent)


def products_kernel(cap, counts, steps, *refs):
    n = sum(counts)
    parts, weights = refs[:n], refs[n : n + 6]
    outs, acc = refs[n + 6 : -1], refs[-1]
    j = pl.program_id(0)
    rows = jnp.concatenate([part[...] for part in parts], axis=0)
    inner = acc.shape[1] // 3

    def add(gate, up, down):
        terms = (
            jnp.dot(rows, gate[...], preferred_element_type=jnp.float32),
            jnp.dot(rows, up[...], preferred_element_type=jnp.float32),
            lax.dot_general(
                rows, down[...], (((1,), (1,)), ((), ())), preferred_element_type=jnp.float32
            ),
        )
        for i, term in enumerate(terms):
            where = slice(i * inner, (i + 1) * inner)

            @pl.when(j == 0)
            def _():
                acc[:, where] = term

            @pl.when(j > 0)
            def _():
                acc[:, where] += term

    @pl.when(j < steps)
    def _():
        add(*weights[:3])

    @pl.when(j >= steps)
    def _():
        add(*weights[3:])

    @pl.when(j == 2 * steps - 1)
    def _():
        row = 0
        for out in outs:
            for b in range(out.shape[0] // cap):
                where = slice(b * cap, (b + 1) * cap)
                out[where, : 2 * inner] = acc[row : row + cap, : 2 * inner]
                out[where, 2 * inner :] = acc[row + cap : row + 2 * cap, 2 * inner :]
                row += 2 * cap


def products(groups, own, other, cap, steps=2):
    parts = [part for group in groups for part in group]
    counts = [len(group) for group in groups]
    chunk, inner = own[0].shape
    tile = chunk // steps
    sizes = [sum(part.shape[0] for part in group) // 2 for group in groups]
    total = sum(part.shape[0] for part in parts)

    def first(j):
        return jnp.minimum(j, steps - 1)

    def second(j):
        return jnp.maximum(j - steps, 0)

    def weight_specs(at):
        return [
            pl.BlockSpec((tile, inner), lambda j: (at(j), 0)),
            pl.BlockSpec((tile, inner), lambda j: (at(j), 0)),
            pl.BlockSpec((inner, tile), lambda j: (0, at(j))),
        ]

    return pl.pallas_call(
        functools.partial(products_kernel, cap, counts, steps),
        grid=(2 * steps,),
        in_specs=[pl.BlockSpec((part.shape[0], tile), lambda j: (0, j)) for part in parts]
        + weight_specs(first)
        + weight_specs(second),
        out_specs=[full((size, 3 * inner)) for size in sizes],
        out_shape=[jax.ShapeDtypeStruct((size, 3 * inner), jnp.float32) for size in sizes],
        scratch_shapes=[pltpu.VMEM((total, 3 * inner), jnp.float32)],
        compiler_params=pltpu.CompilerParams(
            vmem_limit_bytes=40 * MIB, dimension_semantics=("arbitrary",)
        ),
        cost_estimate=pl.CostEstimate(
            flops=2 * total * 6 * chunk * inner, bytes_accessed=12 * chunk * inner, transcendentals=0
        ),
        name="partial_products",
    )(*parts, *own, *other)


def neuron_sums(cap, mine, came, gates):
    total = mine + came
    inner = total.shape[1] // 3
    gate, up, product = total[:, :inner], total[:, inner : 2 * inner], total[:, 2 * inner :]
    terms = jax.nn.silu(gate) * up * (gates[:, None] * product)
    return jnp.sum(terms.reshape(2, -1, inner), axis=1)


def compact_kernel(near_at, far_at, flags, near, far, out):
    j = pl.program_id(0)

    @pl.when(flags[j] == 0)
    def _():
        out[...] = near[...]

    @pl.when(flags[j] != 0)
    def _():
        out[...] = far[...]


def paired_body(tokens, cotangent, route_gate, routes, gate_weight, up_weight, down_weight, dropped):
    experts = lax.axis_size("expert")
    groups = lax.axis_size("dp")
    z, dp, y = lax.axis_index("expert"), lax.axis_index("dp"), lax.axis_index("tensor")
    x, core = dp // 2, dp % 2
    cap = capacity_of(tokens.shape[1], routes.shape[2], experts)
    chunk, inner = gate_weight.shape[1], gate_weight.shape[2]

    def over_core(value):
        return lax.ppermute(value, "dp", [(d, d ^ 1) for d in range(groups)])

    def over_x(value):
        return lax.ppermute(value, "dp", [(d, d ^ 2) for d in range(groups)])

    def over_tensor(value):
        return lax.ppermute(value, "tensor", [(0, 1), (1, 0)])

    def ahead(value, k, dx):
        return lax.ppermute(
            value,
            ("expert", "dp"),
            [
                (e * groups + d, (e + k) % experts * groups + (d ^ (2 * dx)))
                for e in range(experts)
                for d in range(groups)
            ],
        )

    info = jnp.stack([z, x, core, y]).astype(jnp.int32)
    *messages, near, local, slot_gates = pack(
        info, routes, route_gate, tokens, cotangent, experts, cap, 2 * chunk
    )
    own = (gate_weight[0], up_weight[0], down_weight[0])
    order = [(1, 0), (1, 1), (3, 1), (3, 0), (2, 1), (2, 0)]
    window = 2
    came, passed = {}, {}
    came_near = None
    for i, (k, dx) in enumerate(order):
        message = messages[2 * (k - 1) + dx]
        if i >= window:
            message, came[order[i - window]] = lax.optimization_barrier(
                (message, came[order[i - window]])
            )
        came[k, dx] = ahead(message, k, dx)
        if i == 1:
            came_near = over_x(near)
    for at in order:
        passed[at] = over_tensor(came[at])
    other = tuple(over_core(weight) for weight in own)

    all_gates = lax.all_gather(slot_gates[:2, : experts * cap], "expert", axis=0, tiled=False)
    all_gates = all_gates.reshape(experts, 2, experts, cap)

    def gates_of(k):
        source = lax.rem(z + experts - k, experts)
        return lax.dynamic_index_in_dim(all_gates, source, 0, False)[:, k].reshape(2 * cap)

    sums = jnp.zeros((2, inner), jnp.float32)
    kept, sent = products([[local], [near_part for near_part in (came_near,)]], own, other, cap)
    sums = sums + neuron_sums(cap, kept, over_x(sent), gates_of(0))
    for k in (1, 3, 2):
        kept, sent = products(
            [[came[k, 0], passed[k, 0]], [came[k, 1], passed[k, 1]]], own, other, cap
        )
        sums = sums + neuron_sums(cap, kept, over_x(sent), gates_of(k))
    totals = jnp.abs(lax.psum(sums, "dp"))
    saliency = jnp.where(y == 0, totals, totals[::-1])[:, None, :]

    block_of, kept_flag = kept_blocks(dropped)
    pieces_out = KEEP * BLOCK // HALF // 2
    own_blocks = NBLK // 2
    low_pieces = 2 * jnp.sum(kept_flag[:own_blocks].astype(jnp.int32))
    down = own[2].reshape(2 * own_blocks, HALF, chunk)
    most = 3

    def place_of(piece):
        piece = jnp.clip(piece, 0, 2 * KEEP - 1)
        return (block_of[piece // 2] - own_blocks * y) * 2 + piece % 2

    first_sent = jnp.where(y == 0, pieces_out, low_pieces)
    send_at = jnp.clip(place_of(first_sent + jnp.arange(most, dtype=jnp.int32)), 0, 2 * own_blocks - 1)
    down_sent = jnp.concatenate(
        [lax.dynamic_slice_in_dim(down, send_at[i], 1, 0) for i in range(most)], axis=0
    )
    down_came = over_tensor(down_sent)
    target = y * pieces_out + jnp.arange(pieces_out, dtype=jnp.int32)
    far = jnp.where(y == 0, target >= low_pieces, target < low_pieces)
    first_came = jnp.where(y == 0, low_pieces, pieces_out)
    near_at = jnp.clip(place_of(target), 0, 2 * own_blocks - 1)
    far_at = jnp.clip(target - first_came, 0, most - 1)
    compact_down = pl.pallas_call(
        compact_kernel,
        grid_spec=pltpu.PrefetchScalarGridSpec(
            num_scalar_prefetch=3,
            grid=(pieces_out,),
            in_specs=[
                pl.BlockSpec((1, HALF, chunk), lambda j, n, f, w: (n[j], 0, 0)),
                pl.BlockSpec((1, HALF, chunk), lambda j, n, f, w: (f[j], 0, 0)),
            ],
            out_specs=pl.BlockSpec((1, HALF, chunk), lambda j, n, f, w: (j, 0, 0)),
        ),
        out_shape=jax.ShapeDtypeStruct((pieces_out, HALF, chunk), jnp.bfloat16),
        cost_estimate=pl.CostEstimate(flops=0, bytes_accessed=4 * 10**6, transcendentals=0),
        name="kept_rows",
    )(near_at, far_at, far.astype(jnp.int32), down, down_came)
    return saliency, compact_down.reshape(1, pieces_out * HALF, chunk)


def solution(mesh):
    sizes = mesh.shape
    paired = sizes["tensor"] == 2 and sizes["dp"] == 4 and sizes["expert"] == 4
    return jax.shard_map(
        paired_body if paired else general_body,
        mesh=mesh,
        in_specs=(
            P(None, ("expert", "dp"), None),
            P(None, ("expert", "dp"), None),
            P(None, ("expert", "dp"), None),
            P(None, ("expert", "dp"), None),
            P("expert", "dp", "tensor"),
            P("expert", "dp", "tensor"),
            P("expert", "tensor", "dp"),
            P("expert", None),
        ),
        out_specs=(P(None, "expert", "tensor"), P("expert", "tensor", "dp")),
        check_vma=False,
    )
```

```python
import functools

import jax
import jax.numpy as jnp
from jax import lax
from jax.experimental import pallas as pl
from jax.experimental.pallas import tpu as pltpu
from jax.sharding import PartitionSpec as P

BLOCK = 128
NBLK = 8
KEEP = 5
LANES = 128
HALF = 64
MIB = 1 << 20
SMALL = pl.CostEstimate(flops=0, bytes_accessed=0, transcendentals=0)


def capacity_of(tok_rows, top_count, experts):
    return min(tok_rows, max(2, 3 * tok_rows * top_count // (2 * experts)))


def neuron_terms(x_recv, grad_recv, gate_recv, gate_full, up_full, down_full):
    gate_act = jnp.einsum("pscd,df->pscf", x_recv, gate_full, preferred_element_type=jnp.float32)
    up_act = jnp.einsum("pscd,df->pscf", x_recv, up_full, preferred_element_type=jnp.float32)
    hidden = jax.nn.silu(gate_act) * up_act
    product = jnp.einsum("pscd,fd->pscf", grad_recv, down_full, preferred_element_type=jnp.float32)
    hidden_grad = gate_recv.astype(jnp.float32)[..., None] * product
    return jnp.sum(hidden * hidden_grad, axis=(0, 2))


def kept_blocks(dropped):
    blocks = jnp.arange(NBLK, dtype=jnp.int32)
    kept_flag = jnp.all(dropped[0][:, None] != blocks[None, :], axis=0)
    ranking = jnp.cumsum(kept_flag.astype(jnp.int32)) - 1
    ranks = jnp.arange(KEEP, dtype=jnp.int32)
    chosen = kept_flag[None, :] & (ranking[None, :] == ranks[:, None])
    return jnp.sum(jnp.where(chosen, blocks[None, :], 0), axis=1), kept_flag


def general_body(tokens, cotangent, route_gate, routes, gate_weight, up_weight, down_weight, dropped):
    experts = lax.axis_size("expert")
    tensor_count = lax.axis_size("tensor")
    tensor_pos = lax.axis_index("tensor")
    tok_rows = tokens.shape[1]
    capacity = capacity_of(tok_rows, routes.shape[2], experts)
    expert_ids = jnp.arange(experts, dtype=jnp.int32)
    matched = routes[:, :, :, None] == expert_ids
    chosen = jnp.any(matched, axis=2).astype(jnp.float32)
    weight_sum = jnp.sum(
        jnp.where(matched, route_gate.astype(jnp.float32)[:, :, :, None], 0.0), axis=2
    )
    earlier = jnp.cumsum(chosen, axis=1) - chosen
    placing = chosen[..., None] * (earlier[..., None] == jnp.arange(capacity, dtype=jnp.float32))
    slot_gate = jnp.einsum("stec,ste->esc", placing, weight_sum, precision=lax.Precision.HIGHEST)
    gate_slots = slot_gate.astype(jnp.bfloat16)
    placing_half = placing.astype(jnp.bfloat16)
    gate_full = lax.all_gather(gate_weight, "dp", axis=1, tiled=True)[0]
    up_full = lax.all_gather(up_weight, "dp", axis=1, tiled=True)[0]
    down_full = lax.all_gather(down_weight, "dp", axis=2, tiled=True)[0]
    x_slots = jnp.einsum(
        "stec,std->escd", placing_half, tokens, preferred_element_type=jnp.float32
    ).astype(jnp.bfloat16)
    grad_slots = jnp.einsum(
        "stec,std->escd", placing_half, cotangent, preferred_element_type=jnp.float32
    ).astype(jnp.bfloat16)
    partial_terms = neuron_terms(
        lax.all_to_all(x_slots, "expert", split_axis=0, concat_axis=0, tiled=True),
        lax.all_to_all(grad_slots, "expert", split_axis=0, concat_axis=0, tiled=True),
        lax.all_to_all(gate_slots, "expert", split_axis=0, concat_axis=0, tiled=True),
        gate_full,
        up_full,
        down_full,
    )
    totals = lax.psum(partial_terms, "dp")
    saliency = jnp.abs(totals)[:, None, :]
    rows_out = KEEP * BLOCK // tensor_count
    whole_rows = lax.all_gather(down_weight, "tensor", axis=1, tiled=True)[0]
    target_rows = tensor_pos * rows_out + jnp.arange(rows_out, dtype=jnp.int32)
    source_rows = kept_blocks(dropped)[0][target_rows // BLOCK] * BLOCK + target_rows % BLOCK
    compact_down = jnp.take(whole_rows, source_rows, axis=0)[None]
    return (saliency, compact_down)


VMEM = pl.BlockSpec(memory_space=pltpu.VMEM)
HBM = pl.BlockSpec(memory_space=pltpu.HBM)
SMEM = pl.BlockSpec(memory_space=pltpu.SMEM)


def place():
    dp = lax.axis_index("dp")
    return lax.axis_index("expert"), dp // 2, lax.rem(dp, 2), lax.axis_index("tensor")


def pack_kernel(experts, cap, routes, gates, tokens, cotangent, *refs):
    outs, buffers, sems = refs[:-2], refs[-2], refs[-1]
    messages, near, local = outs[:-2], outs[-2], outs[-1]
    z, x, core, y = place()
    rows = tokens.shape[1]
    chunk = near.shape[1] // 2
    steps = [(dx, h) for dx in (1, 0) for h in (0, 1)]
    copies = []
    for i, (dx, h) in enumerate(steps):
        half = x if dx == 0 else 1 - x
        column = pl.multiple_of((2 * half + (core if h == 0 else 1 - core)) * chunk, LANES)
        for j, source in enumerate((tokens, cotangent)):
            copy = pltpu.make_async_copy(
                source.at[:, :, pl.ds(column, chunk)], buffers.at[i, j], sems.at[i, j]
            )
            copy.start()
            copies.append(copy)
    count = experts * cap
    line = lax.broadcasted_iota(jnp.int32, (count, rows), 0)
    ahead = jnp.zeros_like(line)
    for k in range(1, experts):
        ahead = ahead + (line >= k * cap).astype(jnp.int32)
    slot = (line - ahead * cap).astype(jnp.float32)
    expert = z + ahead
    expert = jnp.where(expert >= experts, expert - experts, expert)
    earlier = (
        lax.broadcasted_iota(jnp.int32, (rows, rows), 0)
        < lax.broadcasted_iota(jnp.int32, (rows, rows), 1)
    ).astype(jnp.bfloat16)
    sets, placings, slot_gates = (y, 1 - y), [], []
    for s in sets:
        route, weight = routes[s], gates[s].astype(jnp.float32)
        match = jnp.zeros(line.shape, jnp.float32)
        named = jnp.zeros(line.shape, jnp.float32)
        for k in range(route.shape[0]):
            same = route[k : k + 1, :] == expert
            match = match + jnp.where(same, 1.0, 0.0)
            named = named + jnp.where(same, weight[k : k + 1, :], 0.0)
        rank = jnp.dot(match.astype(jnp.bfloat16), earlier, preferred_element_type=jnp.float32)
        placing = jnp.where(rank == slot, match, 0.0)
        slot_gates.append(jnp.sum(placing * named, axis=1, keepdims=True))
        placings.append(placing.astype(jnp.bfloat16))
    few = -(-cap // 16) * 16
    placings[1] = placings[1][:few]
    blank = jnp.zeros((cap, LANES), jnp.float32)
    extra = slice(2 * chunk, 2 * chunk + LANES)

    def spread(which, k):
        return jnp.broadcast_to(slot_gates[which][k * cap : (k + 1) * cap], (cap, LANES))

    for k in range(1, experts):
        messages[2 * (k - 1)][:, extra] = jnp.concatenate([spread(0, k), blank], axis=0).astype(jnp.bfloat16)
    local[:, extra] = jnp.concatenate([spread(0, 0), blank, spread(1, 0), blank], axis=0).astype(jnp.bfloat16)
    for i, (dx, h) in enumerate(steps):
        copies[2 * i].wait()
        copies[2 * i + 1].wait()
        here = slice(h * chunk, (h + 1) * chunk)
        found = [
            jnp.dot(placing, buffers[i, j, s], preferred_element_type=jnp.float32)
            for s, placing in zip(sets, placings)
            for j in range(2)
        ]
        for k in range(1, experts):
            span = slice(k * cap, (k + 1) * cap)
            messages[2 * (k - 1) + dx][:, here] = jnp.concatenate(
                [found[0][span], found[1][span]], axis=0
            ).astype(jnp.bfloat16)
        (local if dx == 0 else near)[:, here] = jnp.concatenate(
            [part[:cap] for part in found], axis=0
        ).astype(jnp.bfloat16)


def pack(routes, gates, tokens, cotangent, experts, cap, chunk):
    def shape(rows, gated):
        return jax.ShapeDtypeStruct((rows, 2 * chunk + (LANES if gated else 0)), jnp.bfloat16)

    outs = [shape(2 * cap, dx == 0) for _ in range(1, experts) for dx in range(2)]
    outs += [shape(4 * cap, False), shape(4 * cap, True)]
    sets, rows = tokens.shape[:2]
    return pl.pallas_call(
        functools.partial(pack_kernel, experts, cap),
        out_shape=outs,
        in_specs=[VMEM, VMEM, HBM, HBM],
        out_specs=[VMEM] * len(outs),
        scratch_shapes=[
            pltpu.VMEM((4, 2, sets, rows, chunk), jnp.bfloat16),
            pltpu.SemaphoreType.DMA((4, 2)),
        ],
        compiler_params=pltpu.CompilerParams(vmem_limit_bytes=24 * MIB),
        cost_estimate=SMALL,
        name="pack_rows",
    )(routes, gates, tokens, cotangent)


def block_products(parts, weights, cap, put, width=256):
    chunk, inner = weights[0].shape
    left = jnp.concatenate([part[:, :chunk] for part in parts], axis=0)
    right = jnp.concatenate([part[:, chunk : 2 * chunk] for part in parts], axis=0)
    across = (((1,), (1,)), ((), ()))

    def along(columns, own, other):
        return jnp.dot(left, own[:, columns], preferred_element_type=jnp.float32) + jnp.dot(
            right, other[:, columns], preferred_element_type=jnp.float32
        )

    for at in range(0, inner, width):
        columns = slice(at, at + width)
        gate = along(columns, weights[0], weights[3])
        up = along(columns, weights[1], weights[4])
        product = lax.dot_general(
            left, weights[2][columns], across, preferred_element_type=jnp.float32
        ) + lax.dot_general(right, weights[5][columns], across, preferred_element_type=jnp.float32)
        for b in range(left.shape[0] // (2 * cap)):
            row = 2 * cap * b
            put(b, at, gate[row : row + cap], up[row : row + cap], product[row + cap : row + 2 * cap])


def gates_from(parts, cap, chunk):
    found = []
    for part in parts:
        lanes = part[:, 2 * chunk : 2 * chunk + LANES].astype(jnp.float32)
        found += [lanes[b : b + cap] for b in range(0, part.shape[0], 2 * cap)]
    return jnp.concatenate(found, axis=0)


def products_kernel(cap, width, n_sent, n_kept, *refs):
    n = n_sent + n_kept
    parts, weights, outs = refs[:n], refs[n : n + 6], refs[n + 6 :]
    chunk, inner = weights[0].shape
    half = outs[0].shape[0] // cap

    def put(b, at, *terms):
        rows = slice(b % half * cap, (b % half + 1) * cap)
        for i, term in enumerate(terms):
            outs[b // half][rows, i * inner + at : i * inner + at + width] = term

    if n_kept:
        outs[2][...] = gates_from(parts[n_sent:], cap, chunk)
    block_products(parts, weights, cap, put, width)


def products(sent, kept, weights, cap, width=256):
    chunk, inner = weights[0].shape
    half = sum(part.shape[0] for part in sent) // 2
    outs = [jax.ShapeDtypeStruct((half, 3 * inner), jnp.float32)]
    if kept:
        outs += [outs[0], jax.ShapeDtypeStruct((half, LANES), jnp.float32)]
    return pl.pallas_call(
        functools.partial(products_kernel, cap, width, len(sent), len(kept)),
        out_shape=outs,
        in_specs=[VMEM] * (len(sent) + len(kept) + 6),
        out_specs=[VMEM] * len(outs),
        compiler_params=pltpu.CompilerParams(vmem_limit_bytes=16 * MIB),
        cost_estimate=SMALL,
        name="partial_products",
    )(*sent, *kept, *weights)


def neuron_terms_of(gate, up, product, gates):
    return gate / (1.0 + jnp.exp(-gate)) * up * (gates * product)


def in_set_order(mine, other):
    y = lax.axis_index("tensor")
    return jnp.concatenate(
        [jnp.where(y == 0, mine, other), jnp.where(y == 0, other, mine)], axis=0
    )


def finish_kernel(cap, n, *refs):
    out = refs[-1]
    inner = out.shape[1]
    sums = [jnp.zeros((1, inner), jnp.float32)] * 2
    for g in range(n):
        kept, came, gates = refs[3 * g : 3 * g + 3]
        total = kept[...] + came[...]
        terms = neuron_terms_of(
            total[:, :inner], total[:, inner : 2 * inner], total[:, 2 * inner :], gates[:, :1]
        )
        for s in range(2):
            sums[s] = sums[s] + jnp.sum(terms[s * cap : (s + 1) * cap], axis=0, keepdims=True)
    out[...] = in_set_order(*sums)


def finish(groups, cap):
    inner = groups[0][0].shape[1] // 3
    return pl.pallas_call(
        functools.partial(finish_kernel, cap, len(groups)),
        out_shape=jax.ShapeDtypeStruct((2, inner), jnp.float32),
        in_specs=[VMEM] * (3 * len(groups)),
        out_specs=VMEM,
        compiler_params=pltpu.CompilerParams(vmem_limit_bytes=16 * MIB),
        cost_estimate=SMALL,
        name="neuron_sums",
    )(*[value for group in groups for value in group])


def last_kernel(cap, width, mine, other, *refs):
    weights, (came, before, out) = refs[:6], refs[6:]
    chunk, inner = weights[0].shape
    gates = gates_from([mine, other], cap, chunk)
    found = {}

    def put(b, at, *terms):
        rows = slice(b * cap, (b + 1) * cap)
        gate, up, product = (
            term + came[rows, i * inner + at : i * inner + at + width] for i, term in enumerate(terms)
        )
        found[b, at] = jnp.sum(
            neuron_terms_of(gate, up, product, gates[rows, :1]), axis=0, keepdims=True
        )

    block_products([mine, other], weights, cap, put, width)
    for at in range(0, inner, width):
        columns = slice(at, at + width)
        out[:, columns] = before[:, columns] + in_set_order(found[0, at], found[1, at])


def last(mine, other, weights, came, before, cap, width=256):
    chunk, inner = weights[0].shape
    return pl.pallas_call(
        functools.partial(last_kernel, cap, width),
        out_shape=jax.ShapeDtypeStruct((2, inner), jnp.float32),
        in_specs=[VMEM] * 10,
        out_specs=VMEM,
        compiler_params=pltpu.CompilerParams(vmem_limit_bytes=16 * MIB),
        cost_estimate=SMALL,
        name="last_products",
    )(mine, other, *weights, came, before)


def kept_pieces(dropped):
    a, b, c = dropped[0, 0], dropped[0, 1], dropped[0, 2]
    low, high = jnp.minimum(jnp.minimum(a, b), c), jnp.maximum(jnp.maximum(a, b), c)
    middle = a + b + c - low - high

    def place_of(piece):
        block = piece // 2
        for one in (low, middle, high):
            block = block + (block >= one).astype(jnp.int32)
        return 2 * block + lax.rem(piece, 2)

    below = sum((one < NBLK // 2).astype(jnp.int32) for one in (a, b, c))
    return place_of, 2 * (NBLK // 2 - below)


def send_pieces_kernel(dropped, down, out, sems):
    y = lax.axis_index("tensor")
    place_of, low_pieces = kept_pieces(dropped)
    first = jnp.where(y == 0, KEEP, low_pieces)
    copies = []
    for i in range(out.shape[0]):
        piece = jnp.minimum(first + i, 2 * KEEP - 1)
        at = jnp.clip(place_of(piece) - NBLK * y, 0, NBLK - 1)
        copies.append(pltpu.make_async_copy(down.at[at], out.at[i], sems.at[i]))
    for copy in copies:
        copy.start()
    for copy in copies:
        copy.wait()


def keep_pieces_kernel(dropped, down, came, out, sems):
    y = lax.axis_index("tensor")
    place_of, low_pieces = kept_pieces(dropped)
    for i in range(KEEP):
        piece = KEEP * y + i
        is_low = (piece < low_pieces).astype(jnp.int32)
        near = jnp.where(y == 0, is_low, 1 - is_low)
        at = jnp.clip(place_of(piece) - NBLK * y, 0, NBLK - 1)
        far_at = jnp.clip(piece - jnp.where(y == 0, low_pieces, KEEP), 0, came.shape[0] - 1)

        @pl.when(near == 1)
        def _():
            pltpu.make_async_copy(down.at[at], out.at[i], sems.at[i]).start()

        @pl.when(near == 0)
        def _():
            pltpu.make_async_copy(came.at[far_at], out.at[i], sems.at[i]).start()

    for i in range(KEEP):
        pltpu.make_async_copy(down.at[0], out.at[i], sems.at[i]).wait()


def pieces_call(kernel, count, dropped, *sources):
    return pl.pallas_call(
        kernel,
        out_shape=jax.ShapeDtypeStruct((count,) + sources[0].shape[1:], sources[0].dtype),
        in_specs=[SMEM] + [HBM] * len(sources),
        out_specs=VMEM,
        scratch_shapes=[pltpu.SemaphoreType.DMA((count,))],
        compiler_params=pltpu.CompilerParams(vmem_limit_bytes=8 * MIB),
        cost_estimate=SMALL,
        name="kept_rows",
    )(dropped, *sources)


def after(value, *others):
    return lax.optimization_barrier((value,) + others)[0]


def paired_body(tokens, cotangent, route_gate, routes, gate_weight, up_weight, down_weight, dropped):
    experts = lax.axis_size("expert")
    groups = lax.axis_size("dp")
    cap = capacity_of(tokens.shape[1], routes.shape[2], experts)
    chunk = gate_weight.shape[1]

    def over_core(value):
        return lax.ppermute(value, "dp", [(d, d ^ 1) for d in range(groups)])

    def over_x(value):
        return lax.ppermute(value, "dp", [(d, d ^ 2) for d in range(groups)])

    def over_tensor(value):
        return lax.ppermute(value, "tensor", [(0, 1), (1, 0)])

    def ahead(value, k, dx):
        return lax.ppermute(
            value,
            ("expert", "dp"),
            [
                (e * groups + d, (e + k) % experts * groups + (d ^ (2 * dx)))
                for e in range(experts)
                for d in range(groups)
            ],
        )

    *messages, near, local = pack(
        jnp.swapaxes(routes, 1, 2), jnp.swapaxes(route_gate, 1, 2), tokens, cotangent, experts, cap, chunk
    )
    own = (gate_weight[0], up_weight[0], down_weight[0])
    order = [(1, 0), (3, 0), (1, 1), (3, 1), (2, 1), (2, 0)]

    def message(i):
        k, dx = order[i]
        return messages[2 * (k - 1) + dx]

    came, passed = [None] * 6, [None] * 6

    def send(i, *others):
        came[i] = ahead(after(message(i), *others) if others else message(i), *order[i])

    def hand_on(i, *others):
        passed[i] = over_tensor(after(came[i], *others) if others else came[i])

    other = tuple(over_core(weight) for weight in own)
    weights = own + other
    send(0)
    send(1)
    came_near = over_x(after(near, *other))
    send(2, came[0])
    down = own[2].reshape(NBLK, HALF, chunk)
    down_sent = pieces_call(send_pieces_kernel, 3, after(dropped, came[0]), down)
    down_came = over_tensor(down_sent)
    send(3, came[1])
    hand_on(0, down_came)
    hand_on(1)
    terms = {}
    sent, kept, gates = products([came_near], [local], weights, cap)
    terms[0] = (kept, over_x(sent), gates)
    send(4, came[2])
    compact_down = pieces_call(keep_pieces_kernel, KEEP, dropped, down, down_came)
    hand_on(2, compact_down)
    sent, kept, gates = products([came[2], passed[2]], [came[0], passed[0]], weights, cap)
    terms[1] = (kept, over_x(after(sent, terms[0][1])), gates)
    send(5, came[3])
    hand_on(3)
    sent, kept, gates = products([came[3], passed[3]], [came[1], passed[1]], weights, cap)
    terms[3] = (kept, over_x(after(sent, terms[1][1])), gates)
    hand_on(4)
    sums = finish([terms[0], terms[1], terms[3]], cap)
    (sent,) = products([came[4], passed[4]], [], weights, cap)
    hand_on(5, sums)
    totals = last(came[5], passed[5], weights, over_x(sent), sums, cap)
    saliency = jnp.abs(lax.psum(totals, "dp"))[:, None, :]
    return saliency, compact_down.reshape(1, KEEP * HALF, chunk)


def solution(mesh):
    sizes = mesh.shape
    paired = sizes["tensor"] == 2 and sizes["dp"] == 4 and sizes["expert"] == 4
    return jax.shard_map(
        paired_body if paired else general_body,
        mesh=mesh,
        in_specs=(
            P(None, ("expert", "dp"), None),
            P(None, ("expert", "dp"), None),
            P(None, ("expert", "dp"), None),
            P(None, ("expert", "dp"), None),
            P("expert", "dp", "tensor"),
            P("expert", "dp", "tensor"),
            P("expert", "tensor", "dp"),
            P("expert", None),
        ),
        out_specs=(P(None, "expert", "tensor"), P("expert", "tensor", "dp")),
        check_vma=False,
    )
```

```python
import functools

import jax
import jax.numpy as jnp
from jax import lax
from jax.experimental import pallas as pl
from jax.experimental.pallas import tpu as pltpu
from jax.sharding import PartitionSpec as P

BLOCK = 128
NBLK = 8
KEEP = 5
LANES = 128
HALF = 64
MIB = 1 << 20
RAW_LIMIT = 24
ORDER = {
    "c10": ("r1",),
    "c30": ("p21", "x0",),
    "c31": ("n", "p11",),
    "e": ("l",),
    "m": ("a",),
    "n": ("w0", "w1", "w2",),
    "p10": ("d",),
    "p20": ("t",),
    "p31": ("k",),
}
SMALL = pl.CostEstimate(flops=0, bytes_accessed=0, transcendentals=0)


def capacity_of(tok_rows, top_count, experts):
    return min(tok_rows, max(2, 3 * tok_rows * top_count // (2 * experts)))


def neuron_terms(x_recv, grad_recv, gate_recv, gate_full, up_full, down_full):
    gate_act = jnp.einsum("pscd,df->pscf", x_recv, gate_full, preferred_element_type=jnp.float32)
    up_act = jnp.einsum("pscd,df->pscf", x_recv, up_full, preferred_element_type=jnp.float32)
    hidden = jax.nn.silu(gate_act) * up_act
    product = jnp.einsum("pscd,fd->pscf", grad_recv, down_full, preferred_element_type=jnp.float32)
    hidden_grad = gate_recv.astype(jnp.float32)[..., None] * product
    return jnp.sum(hidden * hidden_grad, axis=(0, 2))


def kept_blocks(dropped):
    blocks = jnp.arange(NBLK, dtype=jnp.int32)
    kept_flag = jnp.all(dropped[0][:, None] != blocks[None, :], axis=0)
    ranking = jnp.cumsum(kept_flag.astype(jnp.int32)) - 1
    ranks = jnp.arange(KEEP, dtype=jnp.int32)
    chosen = kept_flag[None, :] & (ranking[None, :] == ranks[:, None])
    return jnp.sum(jnp.where(chosen, blocks[None, :], 0), axis=1), kept_flag


def general_body(tokens, cotangent, route_gate, routes, gate_weight, up_weight, down_weight, dropped):
    experts = lax.axis_size("expert")
    tensor_count = lax.axis_size("tensor")
    tensor_pos = lax.axis_index("tensor")
    tok_rows = tokens.shape[1]
    capacity = capacity_of(tok_rows, routes.shape[2], experts)
    expert_ids = jnp.arange(experts, dtype=jnp.int32)
    matched = routes[:, :, :, None] == expert_ids
    chosen = jnp.any(matched, axis=2).astype(jnp.float32)
    weight_sum = jnp.sum(
        jnp.where(matched, route_gate.astype(jnp.float32)[:, :, :, None], 0.0), axis=2
    )
    earlier = jnp.cumsum(chosen, axis=1) - chosen
    placing = chosen[..., None] * (earlier[..., None] == jnp.arange(capacity, dtype=jnp.float32))
    slot_gate = jnp.einsum("stec,ste->esc", placing, weight_sum, precision=lax.Precision.HIGHEST)
    gate_slots = slot_gate.astype(jnp.bfloat16)
    placing_half = placing.astype(jnp.bfloat16)
    gate_full = lax.all_gather(gate_weight, "dp", axis=1, tiled=True)[0]
    up_full = lax.all_gather(up_weight, "dp", axis=1, tiled=True)[0]
    down_full = lax.all_gather(down_weight, "dp", axis=2, tiled=True)[0]
    x_slots = jnp.einsum(
        "stec,std->escd", placing_half, tokens, preferred_element_type=jnp.float32
    ).astype(jnp.bfloat16)
    grad_slots = jnp.einsum(
        "stec,std->escd", placing_half, cotangent, preferred_element_type=jnp.float32
    ).astype(jnp.bfloat16)
    partial_terms = neuron_terms(
        lax.all_to_all(x_slots, "expert", split_axis=0, concat_axis=0, tiled=True),
        lax.all_to_all(grad_slots, "expert", split_axis=0, concat_axis=0, tiled=True),
        lax.all_to_all(gate_slots, "expert", split_axis=0, concat_axis=0, tiled=True),
        gate_full,
        up_full,
        down_full,
    )
    totals = lax.psum(partial_terms, "dp")
    saliency = jnp.abs(totals)[:, None, :]
    rows_out = KEEP * BLOCK // tensor_count
    whole_rows = lax.all_gather(down_weight, "tensor", axis=1, tiled=True)[0]
    target_rows = tensor_pos * rows_out + jnp.arange(rows_out, dtype=jnp.int32)
    source_rows = kept_blocks(dropped)[0][target_rows // BLOCK] * BLOCK + target_rows % BLOCK
    compact_down = jnp.take(whole_rows, source_rows, axis=0)[None]
    return (saliency, compact_down)


VMEM = pl.BlockSpec(memory_space=pltpu.VMEM)
HBM = pl.BlockSpec(memory_space=pltpu.HBM)
SMEM = pl.BlockSpec(memory_space=pltpu.SMEM)


def place():
    dp = lax.axis_index("dp")
    return lax.axis_index("expert"), dp // 2, lax.rem(dp, 2), lax.axis_index("tensor")


def slots_of(route, weight, experts, cap):
    rows = route[0].shape[1]
    count = len(experts) * cap
    line = lax.broadcasted_iota(jnp.int32, (count, rows), 0)
    expert = jnp.full((count, rows), experts[0], jnp.int32)
    slot = line
    for i, other in enumerate(experts[1:], 1):
        expert = jnp.where(line >= i * cap, other, expert)
        slot = jnp.where(line >= i * cap, line - i * cap, slot)
    earlier = (
        lax.broadcasted_iota(jnp.int32, (rows, rows), 0)
        < lax.broadcasted_iota(jnp.int32, (rows, rows), 1)
    ).astype(jnp.bfloat16)
    match = jnp.zeros((count, rows), jnp.float32)
    named = jnp.zeros((count, rows), jnp.float32)
    for r, w in zip(route, weight):
        same = r == expert
        match = match + jnp.where(same, 1.0, 0.0)
        named = named + jnp.where(same, w, 0.0)
    rank = jnp.dot(match.astype(jnp.bfloat16), earlier, preferred_element_type=jnp.float32)
    placing = jnp.where(rank == slot.astype(jnp.float32), match, 0.0)
    return placing.astype(jnp.bfloat16), jnp.sum(placing * named, axis=1, keepdims=True)


def gate_lanes(columns):
    blocks = []
    for column in columns:
        blocks += [jnp.broadcast_to(column, (column.shape[0], LANES)), jnp.zeros((column.shape[0], LANES), jnp.float32)]
    return jnp.concatenate(blocks, axis=0).astype(jnp.bfloat16)


def rows_of(value):
    return [value[k : k + 1] for k in range(value.shape[0])]


def column_of(x, core, dx, h, chunk):
    half = x if dx == 0 else 1 - x
    return pl.multiple_of((2 * half + (core if h == 0 else 1 - core)) * chunk, LANES)


def raw_kernel(routes, gates, tokens, cotangent, near, far, sems):
    _, x, core, y = place()
    rows = tokens.shape[1]
    chunk = (far.shape[1] - LANES) // 2
    copies = []
    for dx, out in ((1, far), (0, near)):
        for h in range(2):
            for j, source in enumerate((tokens, cotangent)):
                copies.append(
                    pltpu.make_async_copy(
                        source.at[y, :, pl.ds(column_of(x, core, dx, h, chunk), chunk)],
                        out.at[pl.ds(j * rows, rows), pl.ds(h * chunk, chunk)],
                        sems.at[dx, h, j],
                    )
                )
                copies[-1].start()
    line = lax.broadcasted_iota(jnp.int32, (2 * rows, rows), 0)
    notes = jnp.zeros((2 * rows, rows), jnp.float32)
    for i, row in enumerate(rows_of(routes[y].astype(jnp.float32)) + rows_of(gates[y].astype(jnp.float32))):
        notes = jnp.where(line == i, row, notes)
    notes = notes.astype(jnp.bfloat16)
    for out in (far, near):
        out[:, 2 * chunk :] = jnp.zeros((2 * rows, LANES), jnp.bfloat16)
        out[:, 2 * chunk : 2 * chunk + rows] = notes
    for copy in copies:
        copy.wait()


def raw_rows(routes, gates, tokens, cotangent, chunk):
    one = jax.ShapeDtypeStruct((2 * tokens.shape[1], 2 * chunk + LANES), jnp.bfloat16)
    return pl.pallas_call(
        raw_kernel,
        out_shape=[one, one],
        in_specs=[VMEM, VMEM, HBM, HBM],
        out_specs=[VMEM] * 2,
        scratch_shapes=[pltpu.SemaphoreType.DMA((2, 2, 2))],
        compiler_params=pltpu.CompilerParams(vmem_limit_bytes=RAW_LIMIT * MIB),
        cost_estimate=SMALL,
        name="raw_rows",
    )(routes, gates, tokens, cotangent)


def pack_kernel(cap, routes, gates, tokens, cotangent, *refs):
    (next_near, next_far, near, local), (buffers, sems) = refs[:4], refs[4:]
    z, x, core, y = place()
    chunk = near.shape[1] // 2
    steps = [(dx, h) for dx in (0, 1) for h in (0, 1)]
    copies = []
    for i, (dx, h) in enumerate(steps):
        for j, source in enumerate((tokens, cotangent)):
            copies.append(
                pltpu.make_async_copy(
                    source.at[:, :, pl.ds(column_of(x, core, dx, h, chunk), chunk)],
                    buffers.at[i, j],
                    sems.at[i, j],
                )
            )
            copies[-1].start()
    sets, placings, slot_gates = (y, 1 - y), [], []
    for s in sets:
        placing, gate = slots_of(
            rows_of(routes[s]), rows_of(gates[s].astype(jnp.float32)), (z, z ^ 1), cap
        )
        placings.append(placing)
        slot_gates.append(gate)
    next_near[:, 2 * chunk :] = gate_lanes([slot_gates[0][cap:]])
    local[:, 2 * chunk :] = gate_lanes([slot_gates[0][:cap], slot_gates[1][:cap]])
    for i, (dx, h) in enumerate(steps):
        copies[2 * i].wait()
        copies[2 * i + 1].wait()
        here = slice(h * chunk, (h + 1) * chunk)
        found = [
            jnp.dot(placing, buffers[i, j, s], preferred_element_type=jnp.float32)
            for s, placing in zip(sets, placings)
            for j in range(2)
        ]
        (next_near if dx == 0 else next_far)[:, here] = jnp.concatenate(
            [part[cap:] for part in found[:2]], axis=0
        ).astype(jnp.bfloat16)
        (local if dx == 0 else near)[:, here] = jnp.concatenate(
            [part[:cap] for part in found], axis=0
        ).astype(jnp.bfloat16)


def pack(routes, gates, tokens, cotangent, cap, chunk):
    def shape(rows, gated):
        return jax.ShapeDtypeStruct((rows, 2 * chunk + (LANES if gated else 0)), jnp.bfloat16)

    sets, rows = tokens.shape[:2]
    return pl.pallas_call(
        functools.partial(pack_kernel, cap),
        out_shape=[shape(2 * cap, True), shape(2 * cap, False), shape(4 * cap, False), shape(4 * cap, True)],
        in_specs=[VMEM, VMEM, HBM, HBM],
        out_specs=[VMEM] * 4,
        scratch_shapes=[
            pltpu.VMEM((4, 2, sets, rows, chunk), jnp.bfloat16),
            pltpu.SemaphoreType.DMA((4, 2)),
        ],
        compiler_params=pltpu.CompilerParams(vmem_limit_bytes=24 * MIB),
        cost_estimate=SMALL,
        name="pack_rows",
    )(routes, gates, tokens, cotangent)


def unpack_kernel(cap, top, gated, raw, mine, onward):
    z = lax.axis_index("expert")
    rows = raw.shape[0] // 2
    chunk = (raw.shape[1] - LANES) // 2
    notes = raw[:rows, 2 * chunk :].astype(jnp.float32)[:, :rows]
    route = [notes[k : k + 1].astype(jnp.int32) for k in range(top)]
    weight = [notes[top + k : top + k + 1] for k in range(top)]
    placing, gate = slots_of(route, weight, (z, z ^ 1), cap)
    if gated:
        mine[:, 2 * chunk :] = gate_lanes([gate[:cap]])
        onward[:, 2 * chunk :] = gate_lanes([gate[cap:]])
    for h in range(2):
        here = slice(h * chunk, (h + 1) * chunk)
        found = [
            jnp.dot(placing, raw[j * rows : (j + 1) * rows, here], preferred_element_type=jnp.float32)
            for j in range(2)
        ]
        mine[:, here] = jnp.concatenate([part[:cap] for part in found], axis=0).astype(jnp.bfloat16)
        onward[:, here] = jnp.concatenate([part[cap:] for part in found], axis=0).astype(jnp.bfloat16)


def unpack(raw, cap, top, gated):
    one = jax.ShapeDtypeStruct((2 * cap, raw.shape[1] - (0 if gated else LANES)), jnp.bfloat16)
    return pl.pallas_call(
        functools.partial(unpack_kernel, cap, top, gated),
        out_shape=[one, one],
        in_specs=[VMEM],
        out_specs=[VMEM] * 2,
        compiler_params=pltpu.CompilerParams(vmem_limit_bytes=16 * MIB),
        cost_estimate=SMALL,
        name="unpack_rows",
    )(raw)


def block_products(parts, weights, cap, put, width=256):
    chunk, inner = weights[0].shape
    left = jnp.concatenate([part[:, :chunk] for part in parts], axis=0)
    right = jnp.concatenate([part[:, chunk : 2 * chunk] for part in parts], axis=0)
    across = (((1,), (1,)), ((), ()))

    def along(columns, own, other):
        return jnp.dot(left, own[:, columns], preferred_element_type=jnp.float32) + jnp.dot(
            right, other[:, columns], preferred_element_type=jnp.float32
        )

    for at in range(0, inner, width):
        columns = slice(at, at + width)
        gate = along(columns, weights[0], weights[3])
        up = along(columns, weights[1], weights[4])
        product = lax.dot_general(
            left, weights[2][columns], across, preferred_element_type=jnp.float32
        ) + lax.dot_general(right, weights[5][columns], across, preferred_element_type=jnp.float32)
        for b in range(left.shape[0] // (2 * cap)):
            row = 2 * cap * b
            put(b, at, gate[row : row + cap], up[row : row + cap], product[row + cap : row + 2 * cap])


def gates_from(parts, cap, chunk):
    found = []
    for part in parts:
        lanes = part[:, 2 * chunk : 2 * chunk + LANES].astype(jnp.float32)
        found += [lanes[b : b + cap] for b in range(0, part.shape[0], 2 * cap)]
    return jnp.concatenate(found, axis=0)


def products_kernel(cap, width, n_sent, n_kept, *refs):
    n = n_sent + n_kept
    parts, weights, outs = refs[:n], refs[n : n + 6], refs[n + 6 :]
    chunk, inner = weights[0].shape
    half = outs[0].shape[0] // cap

    def put(b, at, *terms):
        rows = slice(b % half * cap, (b % half + 1) * cap)
        for i, term in enumerate(terms):
            outs[b // half][rows, i * inner + at : i * inner + at + width] = term

    if n_kept:
        outs[2][...] = gates_from(parts[n_sent:], cap, chunk)
    block_products(parts, weights, cap, put, width)


def products(sent, kept, weights, cap, width=256):
    chunk, inner = weights[0].shape
    half = sum(part.shape[0] for part in sent) // 2
    outs = [jax.ShapeDtypeStruct((half, 3 * inner), jnp.float32)]
    if kept:
        outs += [outs[0], jax.ShapeDtypeStruct((half, LANES), jnp.float32)]
    return pl.pallas_call(
        functools.partial(products_kernel, cap, width, len(sent), len(kept)),
        out_shape=outs,
        in_specs=[VMEM] * (len(sent) + len(kept) + 6),
        out_specs=[VMEM] * len(outs),
        compiler_params=pltpu.CompilerParams(vmem_limit_bytes=16 * MIB),
        cost_estimate=SMALL,
        name="partial_products",
    )(*sent, *kept, *weights)


def neuron_terms_of(gate, up, product, gates):
    return gate / (1.0 + jnp.exp(-gate)) * up * (gates * product)


def in_set_order(mine, other):
    y = lax.axis_index("tensor")
    return jnp.concatenate(
        [jnp.where(y == 0, mine, other), jnp.where(y == 0, other, mine)], axis=0
    )


def finish_kernel(cap, n, *refs):
    out = refs[-1]
    inner = out.shape[1]
    sums = [jnp.zeros((1, inner), jnp.float32)] * 2
    for g in range(n):
        kept, came, gates = refs[3 * g : 3 * g + 3]
        total = kept[...] + came[...]
        terms = neuron_terms_of(
            total[:, :inner], total[:, inner : 2 * inner], total[:, 2 * inner :], gates[:, :1]
        )
        for s in range(2):
            sums[s] = sums[s] + jnp.sum(terms[s * cap : (s + 1) * cap], axis=0, keepdims=True)
    out[...] = in_set_order(*sums)


def finish(groups, cap):
    inner = groups[0][0].shape[1] // 3
    return pl.pallas_call(
        functools.partial(finish_kernel, cap, len(groups)),
        out_shape=jax.ShapeDtypeStruct((2, inner), jnp.float32),
        in_specs=[VMEM] * (3 * len(groups)),
        out_specs=VMEM,
        compiler_params=pltpu.CompilerParams(vmem_limit_bytes=16 * MIB),
        cost_estimate=SMALL,
        name="neuron_sums",
    )(*[value for group in groups for value in group])


def last_kernel(cap, width, mine, other, *refs):
    weights, (came, before, out) = refs[:6], refs[6:]
    chunk, inner = weights[0].shape
    gates = gates_from([mine, other], cap, chunk)
    found = {}

    def put(b, at, *terms):
        rows = slice(b * cap, (b + 1) * cap)
        gate, up, product = (
            term + came[rows, i * inner + at : i * inner + at + width] for i, term in enumerate(terms)
        )
        found[b, at] = jnp.sum(
            neuron_terms_of(gate, up, product, gates[rows, :1]), axis=0, keepdims=True
        )

    block_products([mine, other], weights, cap, put, width)
    for at in range(0, inner, width):
        columns = slice(at, at + width)
        out[:, columns] = before[:, columns] + in_set_order(found[0, at], found[1, at])


def last(mine, other, weights, came, before, cap, width=256):
    chunk, inner = weights[0].shape
    return pl.pallas_call(
        functools.partial(last_kernel, cap, width),
        out_shape=jax.ShapeDtypeStruct((2, inner), jnp.float32),
        in_specs=[VMEM] * 10,
        out_specs=VMEM,
        compiler_params=pltpu.CompilerParams(vmem_limit_bytes=16 * MIB),
        cost_estimate=SMALL,
        name="last_products",
    )(mine, other, *weights, came, before)


def kept_pieces(dropped):
    a, b, c = dropped[0, 0], dropped[0, 1], dropped[0, 2]
    low, high = jnp.minimum(jnp.minimum(a, b), c), jnp.maximum(jnp.maximum(a, b), c)
    middle = a + b + c - low - high

    def place_of(piece):
        block = piece // 2
        for one in (low, middle, high):
            block = block + (block >= one).astype(jnp.int32)
        return 2 * block + lax.rem(piece, 2)

    below = sum((one < NBLK // 2).astype(jnp.int32) for one in (a, b, c))
    return place_of, 2 * (NBLK // 2 - below)


def send_pieces_kernel(dropped, down, out, sems):
    y = lax.axis_index("tensor")
    place_of, low_pieces = kept_pieces(dropped)
    first = jnp.where(y == 0, KEEP, low_pieces)
    copies = []
    for i in range(out.shape[0]):
        piece = jnp.minimum(first + i, 2 * KEEP - 1)
        at = jnp.clip(place_of(piece) - NBLK * y, 0, NBLK - 1)
        copies.append(pltpu.make_async_copy(down.at[at], out.at[i], sems.at[i]))
    for copy in copies:
        copy.start()
    for copy in copies:
        copy.wait()


def keep_pieces_kernel(dropped, down, came, out, sems):
    y = lax.axis_index("tensor")
    place_of, low_pieces = kept_pieces(dropped)
    for i in range(KEEP):
        piece = KEEP * y + i
        is_low = (piece < low_pieces).astype(jnp.int32)
        near = jnp.where(y == 0, is_low, 1 - is_low)
        at = jnp.clip(place_of(piece) - NBLK * y, 0, NBLK - 1)
        far_at = jnp.clip(piece - jnp.where(y == 0, low_pieces, KEEP), 0, came.shape[0] - 1)

        @pl.when(near == 1)
        def _():
            pltpu.make_async_copy(down.at[at], out.at[i], sems.at[i]).start()

        @pl.when(near == 0)
        def _():
            pltpu.make_async_copy(came.at[far_at], out.at[i], sems.at[i]).start()

    for i in range(KEEP):
        pltpu.make_async_copy(down.at[0], out.at[i], sems.at[i]).wait()


def pieces_call(kernel, count, dropped, *sources):
    return pl.pallas_call(
        kernel,
        out_shape=jax.ShapeDtypeStruct((count,) + sources[0].shape[1:], sources[0].dtype),
        in_specs=[SMEM] + [HBM] * len(sources),
        out_specs=VMEM,
        scratch_shapes=[pltpu.SemaphoreType.DMA((count,))],
        compiler_params=pltpu.CompilerParams(vmem_limit_bytes=8 * MIB),
        cost_estimate=SMALL,
        name="kept_rows",
    )(dropped, *sources)


def paired_body(tokens, cotangent, route_gate, routes, gate_weight, up_weight, down_weight, dropped):
    experts = lax.axis_size("expert")
    groups = lax.axis_size("dp")
    cap = capacity_of(tokens.shape[1], routes.shape[2], experts)
    chunk = gate_weight.shape[1]

    def over_core(value):
        return lax.ppermute(value, "dp", [(d, d ^ 1) for d in range(groups)])

    def over_x(value):
        return lax.ppermute(value, "dp", [(d, d ^ 2) for d in range(groups)])

    def over_tensor(value):
        return lax.ppermute(value, "tensor", [(0, 1), (1, 0)])

    def over_expert(value, bit, dx):
        return lax.ppermute(
            value,
            ("expert", "dp"),
            [
                (e * groups + d, (e ^ bit) * groups + (d ^ (2 * dx)))
                for e in range(experts)
                for d in range(groups)
            ],
        )

    routes_in, gates_in = jnp.swapaxes(routes, 1, 2), jnp.swapaxes(route_gate, 1, 2)
    own = (gate_weight[0], up_weight[0], down_weight[0])
    down = own[2].reshape(NBLK, HALF, chunk)
    made = {}

    def get(name):
        if name not in made:
            made[name] = make(name[0], name[1:])
        return made[name]

    def after(value, name):
        others = tuple(get(one) for one in ORDER.get(name, ()))
        return lax.optimization_barrier((value,) + others)[0] if others else value

    def weights():
        return own + tuple(get("w" + str(i)) for i in range(3))

    def make(kind, rest):
        name = kind + rest
        if kind == "a":
            return raw_rows(routes_in, gates_in, tokens, cotangent, chunk)
        if kind == "m":
            return pack(after(routes_in, name), gates_in, tokens, cotangent, cap, chunk)
        if kind == "l":
            return get("m")[3]
        if kind == "n":
            return over_x(after(get("m")[2], name))
        if kind == "r":
            return over_expert(after(get("a")[int(rest)], name), 2, int(rest))
        if kind == "u":
            return unpack(get("r" + rest), cap, routes.shape[2], rest == "0")
        if kind == "c":
            k, dx = rest
            if k == "2":
                return get("u" + dx)[0]
            value = get("m")[int(dx)] if k == "1" else get("u" + dx)[1]
            return over_expert(after(value, name), 1, int(dx) if k == "1" else 0)
        if kind == "p":
            return over_tensor(after(get("c" + rest), name))
        if kind == "f":
            if rest == "0":
                return products([get("n")], [get("l")], weights(), cap)
            sent = [get("c" + rest + "1"), get("p" + rest + "1")]
            kept = [get("c" + rest + "0"), get("p" + rest + "0")] if rest == "1" else []
            return products(sent, kept, weights(), cap)
        if kind == "v":
            return last(get("c20"), get("p20"), weights(), get("x2"), get("t"), cap)
        if kind == "w":
            return over_core(after(own[int(rest)], name))
        if kind == "f":
            return products_of(rest)
        if kind == "s":
            return get("f" + rest)[0]
        if kind == "x":
            return over_x(after(get("s" + rest), name))
        if kind == "e":
            return pieces_call(send_pieces_kernel, 3, after(dropped, name), down)
        if kind == "d":
            return over_tensor(after(get("e"), name))
        if kind == "k":
            return pieces_call(keep_pieces_kernel, KEEP, dropped, down, get("d"))
        if kind == "t":
            return finish([(get("f" + g)[1], get("x" + g), get("f" + g)[2]) for g in "01"], cap)
        raise ValueError(name)

    totals = last(get("c30"), get("p30"), weights(), get("x3"), get("v"), cap)
    saliency = jnp.abs(lax.psum(totals, "dp"))[:, None, :]
    return saliency, get("k").reshape(1, KEEP * HALF, chunk)


def solution(mesh):
    sizes = mesh.shape
    paired = sizes["tensor"] == 2 and sizes["dp"] == 4 and sizes["expert"] == 4
    return jax.shard_map(
        paired_body if paired else general_body,
        mesh=mesh,
        in_specs=(
            P(None, ("expert", "dp"), None),
            P(None, ("expert", "dp"), None),
            P(None, ("expert", "dp"), None),
            P(None, ("expert", "dp"), None),
            P("expert", "dp", "tensor"),
            P("expert", "dp", "tensor"),
            P("expert", "tensor", "dp"),
            P("expert", None),
        ),
        out_specs=(P(None, "expert", "tensor"), P("expert", "tensor", "dp")),
        check_vma=False,
    )
```

```python
import functools

import jax
import jax.numpy as jnp
from jax import lax
from jax.experimental import pallas as pl
from jax.experimental.pallas import tpu as pltpu
from jax.sharding import PartitionSpec as P

BLOCK = 128
NBLK = 8
KEEP = 5
LANES = 128
HALF = 64
MIB = 1 << 20
RAW_LIMIT = 24
PACK_LIMIT = 24
SENT = 3
ORDER = {
    "c10": ("r1",),
    "c30": ("p21", "x0",),
    "c31": ("p11",),
    "m": ("a",),
    "n": ("w0", "w1", "w2",),
    "p10": ("d",),
    "p30": ("p20", "s2", "t",),
    "p31": ("k",),
    "x3": ("x2",),
}
SMALL = pl.CostEstimate(flops=0, bytes_accessed=0, transcendentals=0)


def capacity_of(tok_rows, top_count, experts):
    return min(tok_rows, max(2, 3 * tok_rows * top_count // (2 * experts)))


def neuron_terms(x_recv, grad_recv, gate_recv, gate_full, up_full, down_full):
    gate_act = jnp.einsum("pscd,df->pscf", x_recv, gate_full, preferred_element_type=jnp.float32)
    up_act = jnp.einsum("pscd,df->pscf", x_recv, up_full, preferred_element_type=jnp.float32)
    hidden = jax.nn.silu(gate_act) * up_act
    product = jnp.einsum("pscd,fd->pscf", grad_recv, down_full, preferred_element_type=jnp.float32)
    hidden_grad = gate_recv.astype(jnp.float32)[..., None] * product
    return jnp.sum(hidden * hidden_grad, axis=(0, 2))


def kept_blocks(dropped):
    blocks = jnp.arange(NBLK, dtype=jnp.int32)
    kept_flag = jnp.all(dropped[0][:, None] != blocks[None, :], axis=0)
    ranking = jnp.cumsum(kept_flag.astype(jnp.int32)) - 1
    ranks = jnp.arange(KEEP, dtype=jnp.int32)
    chosen = kept_flag[None, :] & (ranking[None, :] == ranks[:, None])
    return jnp.sum(jnp.where(chosen, blocks[None, :], 0), axis=1), kept_flag


def general_body(tokens, cotangent, route_gate, routes, gate_weight, up_weight, down_weight, dropped):
    experts = lax.axis_size("expert")
    tensor_count = lax.axis_size("tensor")
    tensor_pos = lax.axis_index("tensor")
    tok_rows = tokens.shape[1]
    capacity = capacity_of(tok_rows, routes.shape[2], experts)
    expert_ids = jnp.arange(experts, dtype=jnp.int32)
    matched = routes[:, :, :, None] == expert_ids
    chosen = jnp.any(matched, axis=2).astype(jnp.float32)
    weight_sum = jnp.sum(
        jnp.where(matched, route_gate.astype(jnp.float32)[:, :, :, None], 0.0), axis=2
    )
    earlier = jnp.cumsum(chosen, axis=1) - chosen
    placing = chosen[..., None] * (earlier[..., None] == jnp.arange(capacity, dtype=jnp.float32))
    slot_gate = jnp.einsum("stec,ste->esc", placing, weight_sum, precision=lax.Precision.HIGHEST)
    gate_slots = slot_gate.astype(jnp.bfloat16)
    placing_half = placing.astype(jnp.bfloat16)
    gate_full = lax.all_gather(gate_weight, "dp", axis=1, tiled=True)[0]
    up_full = lax.all_gather(up_weight, "dp", axis=1, tiled=True)[0]
    down_full = lax.all_gather(down_weight, "dp", axis=2, tiled=True)[0]
    x_slots = jnp.einsum(
        "stec,std->escd", placing_half, tokens, preferred_element_type=jnp.float32
    ).astype(jnp.bfloat16)
    grad_slots = jnp.einsum(
        "stec,std->escd", placing_half, cotangent, preferred_element_type=jnp.float32
    ).astype(jnp.bfloat16)
    partial_terms = neuron_terms(
        lax.all_to_all(x_slots, "expert", split_axis=0, concat_axis=0, tiled=True),
        lax.all_to_all(grad_slots, "expert", split_axis=0, concat_axis=0, tiled=True),
        lax.all_to_all(gate_slots, "expert", split_axis=0, concat_axis=0, tiled=True),
        gate_full,
        up_full,
        down_full,
    )
    totals = lax.psum(partial_terms, "dp")
    saliency = jnp.abs(totals)[:, None, :]
    rows_out = KEEP * BLOCK // tensor_count
    whole_rows = lax.all_gather(down_weight, "tensor", axis=1, tiled=True)[0]
    target_rows = tensor_pos * rows_out + jnp.arange(rows_out, dtype=jnp.int32)
    source_rows = kept_blocks(dropped)[0][target_rows // BLOCK] * BLOCK + target_rows % BLOCK
    compact_down = jnp.take(whole_rows, source_rows, axis=0)[None]
    return (saliency, compact_down)


VMEM = pl.BlockSpec(memory_space=pltpu.VMEM)
HBM = pl.BlockSpec(memory_space=pltpu.HBM)
SMEM = pl.BlockSpec(memory_space=pltpu.SMEM)


def place():
    dp = lax.axis_index("dp")
    return lax.axis_index("expert"), dp // 2, lax.rem(dp, 2), lax.axis_index("tensor")


def slots_of(route, weight, experts, cap):
    rows = route[0].shape[1]
    count = len(experts) * cap
    line = lax.broadcasted_iota(jnp.int32, (count, rows), 0)
    expert = jnp.full((count, rows), experts[0], jnp.int32)
    slot = line
    for i, other in enumerate(experts[1:], 1):
        expert = jnp.where(line >= i * cap, other, expert)
        slot = jnp.where(line >= i * cap, line - i * cap, slot)
    earlier = (
        lax.broadcasted_iota(jnp.int32, (rows, rows), 0)
        < lax.broadcasted_iota(jnp.int32, (rows, rows), 1)
    ).astype(jnp.bfloat16)
    match = jnp.zeros((count, rows), jnp.float32)
    named = jnp.zeros((count, rows), jnp.float32)
    for r, w in zip(route, weight):
        same = r == expert
        match = match + jnp.where(same, 1.0, 0.0)
        named = named + jnp.where(same, w, 0.0)
    rank = jnp.dot(match.astype(jnp.bfloat16), earlier, preferred_element_type=jnp.float32)
    placing = jnp.where(rank == slot.astype(jnp.float32), match, 0.0)
    return placing.astype(jnp.bfloat16), jnp.sum(placing * named, axis=1, keepdims=True)


def gate_lanes(columns):
    blocks = []
    for column in columns:
        blocks += [jnp.broadcast_to(column, (column.shape[0], LANES)), jnp.zeros((column.shape[0], LANES), jnp.float32)]
    return jnp.concatenate(blocks, axis=0).astype(jnp.bfloat16)


def rows_of(value):
    return [value[k : k + 1] for k in range(value.shape[0])]


def column_of(x, core, dx, h, chunk):
    half = x if dx == 0 else 1 - x
    return pl.multiple_of((2 * half + (core if h == 0 else 1 - core)) * chunk, LANES)


def raw_kernel(routes, gates, tokens, cotangent, near, far, sems):
    _, x, core, y = place()
    rows = tokens.shape[1]
    chunk = (far.shape[1] - LANES) // 2
    copies = []
    for dx, out in ((1, far), (0, near)):
        for h in range(2):
            for j, source in enumerate((tokens, cotangent)):
                copies.append(
                    pltpu.make_async_copy(
                        source.at[y, :, pl.ds(column_of(x, core, dx, h, chunk), chunk)],
                        out.at[pl.ds(j * rows, rows), pl.ds(h * chunk, chunk)],
                        sems.at[dx, h, j],
                    )
                )
                copies[-1].start()
    line = lax.broadcasted_iota(jnp.int32, (2 * rows, rows), 0)
    notes = jnp.zeros((2 * rows, rows), jnp.float32)
    for i, row in enumerate(rows_of(routes[y].astype(jnp.float32)) + rows_of(gates[y].astype(jnp.float32))):
        notes = jnp.where(line == i, row, notes)
    notes = notes.astype(jnp.bfloat16)
    for out in (far, near):
        out[:, 2 * chunk :] = jnp.zeros((2 * rows, LANES), jnp.bfloat16)
        out[:, 2 * chunk : 2 * chunk + rows] = notes
    for copy in copies:
        copy.wait()


def raw_rows(routes, gates, tokens, cotangent, chunk):
    one = jax.ShapeDtypeStruct((2 * tokens.shape[1], 2 * chunk + LANES), jnp.bfloat16)
    return pl.pallas_call(
        raw_kernel,
        out_shape=[one, one],
        in_specs=[VMEM, VMEM, HBM, HBM],
        out_specs=[VMEM] * 2,
        scratch_shapes=[pltpu.SemaphoreType.DMA((2, 2, 2))],
        compiler_params=pltpu.CompilerParams(vmem_limit_bytes=RAW_LIMIT * MIB),
        cost_estimate=SMALL,
        name="raw_rows",
    )(routes, gates, tokens, cotangent)


def pack_kernel(cap, routes, gates, tokens, cotangent, dropped, down, *refs):
    (next_near, next_far, near, local, pieces), (buffers, sems, piece_sems) = refs[:5], refs[5:]
    z, x, core, y = place()
    chunk = near.shape[1] // 2
    steps = [(dx, h) for dx in (0, 1) for h in (0, 1)]
    copies = []
    for i, (dx, h) in enumerate(steps):
        for j, source in enumerate((tokens, cotangent)):
            copies.append(
                pltpu.make_async_copy(
                    source.at[:, :, pl.ds(column_of(x, core, dx, h, chunk), chunk)],
                    buffers.at[i, j],
                    sems.at[i, j],
                )
            )
            copies[-1].start()
    piece_copies = pieces_to_send(dropped, down, pieces, piece_sems)
    for copy in piece_copies:
        copy.start()
    sets, placings, slot_gates = (y, 1 - y), [], []
    for s in sets:
        placing, gate = slots_of(
            rows_of(routes[s]), rows_of(gates[s].astype(jnp.float32)), (z, z ^ 1), cap
        )
        placings.append(placing)
        slot_gates.append(gate)
    next_near[:, 2 * chunk :] = gate_lanes([slot_gates[0][cap:]])
    local[:, 2 * chunk :] = gate_lanes([slot_gates[0][:cap], slot_gates[1][:cap]])
    for i, (dx, h) in enumerate(steps):
        copies[2 * i].wait()
        copies[2 * i + 1].wait()
        here = slice(h * chunk, (h + 1) * chunk)
        found = [
            jnp.dot(placing, buffers[i, j, s], preferred_element_type=jnp.float32)
            for s, placing in zip(sets, placings)
            for j in range(2)
        ]
        (next_near if dx == 0 else next_far)[:, here] = jnp.concatenate(
            [part[cap:] for part in found[:2]], axis=0
        ).astype(jnp.bfloat16)
        (local if dx == 0 else near)[:, here] = jnp.concatenate(
            [part[:cap] for part in found], axis=0
        ).astype(jnp.bfloat16)
    for copy in piece_copies:
        copy.wait()


def pack(routes, gates, tokens, cotangent, dropped, down, cap):
    def shape(rows, gated):
        return jax.ShapeDtypeStruct((rows, 2 * chunk + (LANES if gated else 0)), jnp.bfloat16)

    sets, rows = tokens.shape[:2]
    half, chunk = down.shape[1:]
    outs = [shape(2 * cap, True), shape(2 * cap, False), shape(4 * cap, False), shape(4 * cap, True)]
    return pl.pallas_call(
        functools.partial(pack_kernel, cap),
        out_shape=outs + [jax.ShapeDtypeStruct((SENT, half, chunk), down.dtype)],
        in_specs=[VMEM, VMEM, HBM, HBM, SMEM, HBM],
        out_specs=[VMEM] * 5,
        scratch_shapes=[
            pltpu.VMEM((4, 2, sets, rows, chunk), jnp.bfloat16),
            pltpu.SemaphoreType.DMA((4, 2)),
            pltpu.SemaphoreType.DMA((SENT,)),
        ],
        compiler_params=pltpu.CompilerParams(vmem_limit_bytes=PACK_LIMIT * MIB),
        cost_estimate=SMALL,
        name="pack_rows",
    )(routes, gates, tokens, cotangent, dropped, down)


def unpack_kernel(cap, top, gated, raw, mine, onward):
    z = lax.axis_index("expert")
    rows = raw.shape[0] // 2
    chunk = (raw.shape[1] - LANES) // 2
    notes = raw[:rows, 2 * chunk :].astype(jnp.float32)[:, :rows]
    route = [notes[k : k + 1].astype(jnp.int32) for k in range(top)]
    weight = [notes[top + k : top + k + 1] for k in range(top)]
    placing, gate = slots_of(route, weight, (z, z ^ 1), cap)
    if gated:
        mine[:, 2 * chunk :] = gate_lanes([gate[:cap]])
        onward[:, 2 * chunk :] = gate_lanes([gate[cap:]])
    for h in range(2):
        here = slice(h * chunk, (h + 1) * chunk)
        found = [
            jnp.dot(placing, raw[j * rows : (j + 1) * rows, here], preferred_element_type=jnp.float32)
            for j in range(2)
        ]
        mine[:, here] = jnp.concatenate([part[:cap] for part in found], axis=0).astype(jnp.bfloat16)
        onward[:, here] = jnp.concatenate([part[cap:] for part in found], axis=0).astype(jnp.bfloat16)


def unpack(raw, cap, top, gated):
    one = jax.ShapeDtypeStruct((2 * cap, raw.shape[1] - (0 if gated else LANES)), jnp.bfloat16)
    return pl.pallas_call(
        functools.partial(unpack_kernel, cap, top, gated),
        out_shape=[one, one],
        in_specs=[VMEM],
        out_specs=[VMEM] * 2,
        compiler_params=pltpu.CompilerParams(vmem_limit_bytes=16 * MIB),
        cost_estimate=SMALL,
        name="unpack_rows",
    )(raw)


def block_products(parts, weights, cap, put, width=256):
    chunk, inner = weights[0].shape
    left = jnp.concatenate([part[:, :chunk] for part in parts], axis=0)
    right = jnp.concatenate([part[:, chunk : 2 * chunk] for part in parts], axis=0)
    across = (((1,), (1,)), ((), ()))

    def along(columns, own, other):
        return jnp.dot(left, own[:, columns], preferred_element_type=jnp.float32) + jnp.dot(
            right, other[:, columns], preferred_element_type=jnp.float32
        )

    for at in range(0, inner, width):
        columns = slice(at, at + width)
        gate = along(columns, weights[0], weights[3])
        up = along(columns, weights[1], weights[4])
        product = lax.dot_general(
            left, weights[2][columns], across, preferred_element_type=jnp.float32
        ) + lax.dot_general(right, weights[5][columns], across, preferred_element_type=jnp.float32)
        for b in range(left.shape[0] // (2 * cap)):
            row = 2 * cap * b
            put(b, at, gate[row : row + cap], up[row : row + cap], product[row + cap : row + 2 * cap])


def gates_from(parts, cap, chunk):
    found = []
    for part in parts:
        lanes = part[:, 2 * chunk : 2 * chunk + LANES].astype(jnp.float32)
        found += [lanes[b : b + cap] for b in range(0, part.shape[0], 2 * cap)]
    return jnp.concatenate(found, axis=0)


def products_kernel(cap, width, n_sent, n_kept, *refs):
    n = n_sent + n_kept
    parts, weights, outs = refs[:n], refs[n : n + 6], refs[n + 6 :]
    chunk, inner = weights[0].shape
    half = outs[0].shape[0] // cap

    def put(b, at, *terms):
        rows = slice(b % half * cap, (b % half + 1) * cap)
        for i, term in enumerate(terms):
            outs[b // half][rows, i * inner + at : i * inner + at + width] = term

    if n_kept:
        outs[2][...] = gates_from(parts[n_sent:], cap, chunk)
    block_products(parts, weights, cap, put, width)


def products(sent, kept, weights, cap, width=256):
    chunk, inner = weights[0].shape
    half = sum(part.shape[0] for part in sent) // 2
    outs = [jax.ShapeDtypeStruct((half, 3 * inner), jnp.float32)]
    if kept:
        outs += [outs[0], jax.ShapeDtypeStruct((half, LANES), jnp.float32)]
    return pl.pallas_call(
        functools.partial(products_kernel, cap, width, len(sent), len(kept)),
        out_shape=outs,
        in_specs=[VMEM] * (len(sent) + len(kept) + 6),
        out_specs=[VMEM] * len(outs),
        compiler_params=pltpu.CompilerParams(vmem_limit_bytes=16 * MIB),
        cost_estimate=SMALL,
        name="partial_products",
    )(*sent, *kept, *weights)


def neuron_terms_of(gate, up, product, gates):
    return gate / (1.0 + jnp.exp(-gate)) * up * (gates * product)


def in_set_order(mine, other):
    y = lax.axis_index("tensor")
    return jnp.concatenate(
        [jnp.where(y == 0, mine, other), jnp.where(y == 0, other, mine)], axis=0
    )


def finish_kernel(cap, n, *refs):
    out = refs[-1]
    inner = out.shape[2]
    sums = [jnp.zeros((1, inner), jnp.float32)] * 2
    for g in range(n):
        kept, came, gates = refs[3 * g : 3 * g + 3]
        total = kept[...] + came[...]
        terms = neuron_terms_of(
            total[:, :inner], total[:, inner : 2 * inner], total[:, 2 * inner :], gates[:, :1]
        )
        for s in range(2):
            sums[s] = sums[s] + jnp.sum(terms[s * cap : (s + 1) * cap], axis=0, keepdims=True)
    out[:, 0, :] = in_set_order(*sums)


def finish(groups, cap):
    inner = groups[0][0].shape[1] // 3
    return pl.pallas_call(
        functools.partial(finish_kernel, cap, len(groups)),
        out_shape=jax.ShapeDtypeStruct((2, 1, inner), jnp.float32),
        in_specs=[VMEM] * (3 * len(groups)),
        out_specs=VMEM,
        compiler_params=pltpu.CompilerParams(vmem_limit_bytes=16 * MIB),
        cost_estimate=SMALL,
        name="neuron_sums",
    )(*[value for group in groups for value in group])


def last_kernel(cap, width, mine, other, *refs):
    weights, (came, before, out) = refs[:6], refs[6:]
    chunk, inner = weights[0].shape
    gates = gates_from([mine, other], cap, chunk)
    found = {}

    def put(b, at, *terms):
        rows = slice(b * cap, (b + 1) * cap)
        gate, up, product = (
            term + came[rows, i * inner + at : i * inner + at + width] for i, term in enumerate(terms)
        )
        found[b, at] = jnp.sum(
            neuron_terms_of(gate, up, product, gates[rows, :1]), axis=0, keepdims=True
        )

    block_products([mine, other], weights, cap, put, width)
    for at in range(0, inner, width):
        columns = slice(at, at + width)
        out[:, 0, columns] = before[:, 0, columns] + in_set_order(found[0, at], found[1, at])


def last(mine, other, weights, came, before, cap, width=256):
    chunk, inner = weights[0].shape
    return pl.pallas_call(
        functools.partial(last_kernel, cap, width),
        out_shape=jax.ShapeDtypeStruct((2, 1, inner), jnp.float32),
        in_specs=[VMEM] * 10,
        out_specs=VMEM,
        compiler_params=pltpu.CompilerParams(vmem_limit_bytes=16 * MIB),
        cost_estimate=SMALL,
        name="last_products",
    )(mine, other, *weights, came, before)


def kept_pieces(dropped):
    a, b, c = dropped[0, 0], dropped[0, 1], dropped[0, 2]
    low, high = jnp.minimum(jnp.minimum(a, b), c), jnp.maximum(jnp.maximum(a, b), c)
    middle = a + b + c - low - high

    def place_of(piece):
        block = piece // 2
        for one in (low, middle, high):
            block = block + (block >= one).astype(jnp.int32)
        return 2 * block + lax.rem(piece, 2)

    below = sum((one < NBLK // 2).astype(jnp.int32) for one in (a, b, c))
    return place_of, 2 * (NBLK // 2 - below)


def pieces_to_send(dropped, down, out, sems):
    y = lax.axis_index("tensor")
    place_of, low_pieces = kept_pieces(dropped)
    first = jnp.where(y == 0, KEEP, low_pieces)
    copies = []
    for i in range(out.shape[0]):
        piece = jnp.minimum(first + i, 2 * KEEP - 1)
        at = jnp.clip(place_of(piece) - NBLK * y, 0, NBLK - 1)
        copies.append(pltpu.make_async_copy(down.at[at], out.at[i], sems.at[i]))
    return copies


def keep_pieces_kernel(dropped, down, came, out, sems):
    y = lax.axis_index("tensor")
    place_of, low_pieces = kept_pieces(dropped)
    for i in range(KEEP):
        piece = KEEP * y + i
        is_low = (piece < low_pieces).astype(jnp.int32)
        near = jnp.where(y == 0, is_low, 1 - is_low)
        at = jnp.clip(place_of(piece) - NBLK * y, 0, NBLK - 1)
        far_at = jnp.clip(piece - jnp.where(y == 0, low_pieces, KEEP), 0, came.shape[0] - 1)

        @pl.when(near == 1)
        def _():
            pltpu.make_async_copy(down.at[at], out.at[i], sems.at[i]).start()

        @pl.when(near == 0)
        def _():
            pltpu.make_async_copy(came.at[far_at], out.at[i], sems.at[i]).start()

    for i in range(KEEP):
        pltpu.make_async_copy(down.at[0], out.at[i], sems.at[i]).wait()


def keep_pieces(dropped, down, came):
    return pl.pallas_call(
        keep_pieces_kernel,
        out_shape=jax.ShapeDtypeStruct((KEEP,) + down.shape[1:], down.dtype),
        in_specs=[SMEM, HBM, HBM],
        out_specs=VMEM,
        scratch_shapes=[pltpu.SemaphoreType.DMA((KEEP,))],
        compiler_params=pltpu.CompilerParams(vmem_limit_bytes=8 * MIB),
        cost_estimate=SMALL,
        name="kept_rows",
    )(dropped, down, came)


def paired_body(tokens, cotangent, route_gate, routes, gate_weight, up_weight, down_weight, dropped):
    experts = lax.axis_size("expert")
    groups = lax.axis_size("dp")
    cap = capacity_of(tokens.shape[1], routes.shape[2], experts)
    chunk = gate_weight.shape[1]

    def over_core(value):
        return lax.ppermute(value, "dp", [(d, d ^ 1) for d in range(groups)])

    def over_x(value):
        return lax.ppermute(value, "dp", [(d, d ^ 2) for d in range(groups)])

    def over_tensor(value):
        return lax.ppermute(value, "tensor", [(0, 1), (1, 0)])

    def over_expert(value, bit, dx):
        return lax.ppermute(
            value,
            ("expert", "dp"),
            [
                (e * groups + d, (e ^ bit) * groups + (d ^ (2 * dx)))
                for e in range(experts)
                for d in range(groups)
            ],
        )

    routes_in, gates_in = jnp.swapaxes(routes, 1, 2), jnp.swapaxes(route_gate, 1, 2)
    own = (gate_weight[0], up_weight[0], down_weight[0])
    down = own[2].reshape(NBLK, HALF, chunk)
    made = {}

    def get(name):
        if name not in made:
            made[name] = make(name[0], name[1:])
        return made[name]

    def after(value, name):
        others = tuple(get(one) for one in ORDER.get(name, ()))
        return lax.optimization_barrier((value,) + others)[0] if others else value

    def weights():
        return own + tuple(get("w" + str(i)) for i in range(3))

    def make(kind, rest):
        name = kind + rest
        if kind == "a":
            return raw_rows(routes_in, gates_in, tokens, cotangent, chunk)
        if kind == "m":
            return pack(after(routes_in, name), gates_in, tokens, cotangent, dropped, down, cap)
        if kind == "l":
            return get("m")[3]
        if kind == "n":
            return over_x(after(get("m")[2], name))
        if kind == "r":
            return over_expert(after(get("a")[int(rest)], name), 2, int(rest))
        if kind == "u":
            return unpack(get("r" + rest), cap, routes.shape[2], rest == "0")
        if kind == "c":
            k, dx = rest
            if k == "2":
                return get("u" + dx)[0]
            value = get("m")[int(dx)] if k == "1" else get("u" + dx)[1]
            return over_expert(after(value, name), 1, int(dx) if k == "1" else 0)
        if kind == "p":
            return over_tensor(after(get("c" + rest), name))
        if kind == "f":
            if rest == "0":
                return products([get("n")], [get("l")], weights(), cap)
            sent = [get("c" + rest + "1"), get("p" + rest + "1")]
            kept = [get("c" + rest + "0"), get("p" + rest + "0")] if rest == "1" else []
            return products(sent, kept, weights(), cap)
        if kind == "v":
            return last(get("c20"), get("p20"), weights(), get("x2"), get("t"), cap)
        if kind == "w":
            return over_core(after(own[int(rest)], name))
        if kind == "f":
            return products_of(rest)
        if kind == "s":
            return get("f" + rest)[0]
        if kind == "x":
            return over_x(after(get("s" + rest), name))
        if kind == "d":
            return over_tensor(after(get("m")[4], name))
        if kind == "k":
            return keep_pieces(dropped, down, get("d"))
        if kind == "t":
            return finish([(get("f" + g)[1], get("x" + g), get("f" + g)[2]) for g in "01"], cap)
        raise ValueError(name)

    totals = last(get("c30"), get("p30"), weights(), get("x3"), get("v"), cap)
    saliency = jnp.abs(lax.psum(totals, "dp"))
    return saliency, get("k").reshape(1, KEEP * HALF, chunk)


def solution(mesh):
    sizes = mesh.shape
    paired = sizes["tensor"] == 2 and sizes["dp"] == 4 and sizes["expert"] == 4
    return jax.shard_map(
        paired_body if paired else general_body,
        mesh=mesh,
        in_specs=(
            P(None, ("expert", "dp"), None),
            P(None, ("expert", "dp"), None),
            P(None, ("expert", "dp"), None),
            P(None, ("expert", "dp"), None),
            P("expert", "dp", "tensor"),
            P("expert", "dp", "tensor"),
            P("expert", "tensor", "dp"),
            P("expert", None),
        ),
        out_specs=(P(None, "expert", "tensor"), P("expert", "tensor", "dp")),
        check_vma=False,
    )
```

```python
import functools

import jax
import jax.numpy as jnp
from jax import lax
from jax.experimental import pallas as pl
from jax.experimental.pallas import tpu as pltpu
from jax.sharding import PartitionSpec as P

BLOCK = 128
NBLK = 8
KEEP = 5
LANES = 128
HALF = 64
MIB = 1 << 20
RAW_LIMIT = 24
PACK_LIMIT = 24
SENT = 3
ORDER = {
    "c10": ("r1",),
    "c30": ("p21", "x0",),
    "c31": ("p11",),
    "m": ("a",),
    "n": ("w0", "w1", "w2",),
    "p10": ("d",),
    "p30": ("p20", "s2", "t",),
    "p31": ("k",),
    "x3": ("x2",),
}
SMALL = pl.CostEstimate(flops=0, bytes_accessed=0, transcendentals=0)


def capacity_of(tok_rows, top_count, experts):
    return min(tok_rows, max(2, 3 * tok_rows * top_count // (2 * experts)))


def neuron_terms(x_recv, grad_recv, gate_recv, gate_full, up_full, down_full):
    gate_act = jnp.einsum("pscd,df->pscf", x_recv, gate_full, preferred_element_type=jnp.float32)
    up_act = jnp.einsum("pscd,df->pscf", x_recv, up_full, preferred_element_type=jnp.float32)
    hidden = jax.nn.silu(gate_act) * up_act
    product = jnp.einsum("pscd,fd->pscf", grad_recv, down_full, preferred_element_type=jnp.float32)
    hidden_grad = gate_recv.astype(jnp.float32)[..., None] * product
    return jnp.sum(hidden * hidden_grad, axis=(0, 2))


def kept_blocks(dropped):
    blocks = jnp.arange(NBLK, dtype=jnp.int32)
    kept_flag = jnp.all(dropped[0][:, None] != blocks[None, :], axis=0)
    ranking = jnp.cumsum(kept_flag.astype(jnp.int32)) - 1
    ranks = jnp.arange(KEEP, dtype=jnp.int32)
    chosen = kept_flag[None, :] & (ranking[None, :] == ranks[:, None])
    return jnp.sum(jnp.where(chosen, blocks[None, :], 0), axis=1), kept_flag


def general_body(tokens, cotangent, route_gate, routes, gate_weight, up_weight, down_weight, dropped):
    experts = lax.axis_size("expert")
    tensor_count = lax.axis_size("tensor")
    tensor_pos = lax.axis_index("tensor")
    tok_rows = tokens.shape[1]
    capacity = capacity_of(tok_rows, routes.shape[2], experts)
    expert_ids = jnp.arange(experts, dtype=jnp.int32)
    matched = routes[:, :, :, None] == expert_ids
    chosen = jnp.any(matched, axis=2).astype(jnp.float32)
    weight_sum = jnp.sum(
        jnp.where(matched, route_gate.astype(jnp.float32)[:, :, :, None], 0.0), axis=2
    )
    earlier = jnp.cumsum(chosen, axis=1) - chosen
    placing = chosen[..., None] * (earlier[..., None] == jnp.arange(capacity, dtype=jnp.float32))
    slot_gate = jnp.einsum("stec,ste->esc", placing, weight_sum, precision=lax.Precision.HIGHEST)
    gate_slots = slot_gate.astype(jnp.bfloat16)
    placing_half = placing.astype(jnp.bfloat16)
    gate_full = lax.all_gather(gate_weight, "dp", axis=1, tiled=True)[0]
    up_full = lax.all_gather(up_weight, "dp", axis=1, tiled=True)[0]
    down_full = lax.all_gather(down_weight, "dp", axis=2, tiled=True)[0]
    x_slots = jnp.einsum(
        "stec,std->escd", placing_half, tokens, preferred_element_type=jnp.float32
    ).astype(jnp.bfloat16)
    grad_slots = jnp.einsum(
        "stec,std->escd", placing_half, cotangent, preferred_element_type=jnp.float32
    ).astype(jnp.bfloat16)
    partial_terms = neuron_terms(
        lax.all_to_all(x_slots, "expert", split_axis=0, concat_axis=0, tiled=True),
        lax.all_to_all(grad_slots, "expert", split_axis=0, concat_axis=0, tiled=True),
        lax.all_to_all(gate_slots, "expert", split_axis=0, concat_axis=0, tiled=True),
        gate_full,
        up_full,
        down_full,
    )
    totals = lax.psum(partial_terms, "dp")
    saliency = jnp.abs(totals)[:, None, :]
    rows_out = KEEP * BLOCK // tensor_count
    whole_rows = lax.all_gather(down_weight, "tensor", axis=1, tiled=True)[0]
    target_rows = tensor_pos * rows_out + jnp.arange(rows_out, dtype=jnp.int32)
    source_rows = kept_blocks(dropped)[0][target_rows // BLOCK] * BLOCK + target_rows % BLOCK
    compact_down = jnp.take(whole_rows, source_rows, axis=0)[None]
    return (saliency, compact_down)


VMEM = pl.BlockSpec(memory_space=pltpu.VMEM)
HBM = pl.BlockSpec(memory_space=pltpu.HBM)
SMEM = pl.BlockSpec(memory_space=pltpu.SMEM)


def place():
    dp = lax.axis_index("dp")
    return lax.axis_index("expert"), dp // 2, lax.rem(dp, 2), lax.axis_index("tensor")


def slots_of(route, weight, experts, cap):
    rows = route[0].shape[1]
    count = len(experts) * cap
    line = lax.broadcasted_iota(jnp.int32, (count, rows), 0)
    expert = jnp.full((count, rows), experts[0], jnp.int32)
    slot = line
    for i, other in enumerate(experts[1:], 1):
        expert = jnp.where(line >= i * cap, other, expert)
        slot = jnp.where(line >= i * cap, line - i * cap, slot)
    earlier = (
        lax.broadcasted_iota(jnp.int32, (rows, rows), 0)
        < lax.broadcasted_iota(jnp.int32, (rows, rows), 1)
    ).astype(jnp.bfloat16)
    match = jnp.zeros((count, rows), jnp.float32)
    named = jnp.zeros((count, rows), jnp.float32)
    for r, w in zip(route, weight):
        same = r == expert
        match = match + jnp.where(same, 1.0, 0.0)
        named = named + jnp.where(same, w, 0.0)
    rank = jnp.dot(match.astype(jnp.bfloat16), earlier, preferred_element_type=jnp.float32)
    placing = jnp.where(rank == slot.astype(jnp.float32), match, 0.0)
    return placing.astype(jnp.bfloat16), jnp.sum(placing * named, axis=1, keepdims=True)


def gate_lanes(columns):
    blocks = []
    for column in columns:
        blocks += [jnp.broadcast_to(column, (column.shape[0], LANES)), jnp.zeros((column.shape[0], LANES), jnp.float32)]
    return jnp.concatenate(blocks, axis=0).astype(jnp.bfloat16)


def rows_of(value):
    return [value[k : k + 1] for k in range(value.shape[0])]


def column_of(x, core, dx, h, chunk):
    half = x if dx == 0 else 1 - x
    return pl.multiple_of((2 * half + (core if h == 0 else 1 - core)) * chunk, LANES)


def raw_kernel(routes, gates, tokens, cotangent, near, far, sems):
    _, x, core, y = place()
    rows = tokens.shape[1]
    chunk = (far.shape[1] - LANES) // 2
    copies = []
    for dx, out in ((1, far), (0, near)):
        for h in range(2):
            for j, source in enumerate((tokens, cotangent)):
                copies.append(
                    pltpu.make_async_copy(
                        source.at[y, :, pl.ds(column_of(x, core, dx, h, chunk), chunk)],
                        out.at[pl.ds(j * rows, rows), pl.ds(h * chunk, chunk)],
                        sems.at[dx, h, j],
                    )
                )
                copies[-1].start()
    line = lax.broadcasted_iota(jnp.int32, (2 * rows, rows), 0)
    notes = jnp.zeros((2 * rows, rows), jnp.float32)
    for i, row in enumerate(rows_of(routes[y].astype(jnp.float32)) + rows_of(gates[y].astype(jnp.float32))):
        notes = jnp.where(line == i, row, notes)
    notes = notes.astype(jnp.bfloat16)
    for out in (far, near):
        out[:, 2 * chunk :] = jnp.zeros((2 * rows, LANES), jnp.bfloat16)
        out[:, 2 * chunk : 2 * chunk + rows] = notes
    for copy in copies:
        copy.wait()


def raw_rows(routes, gates, tokens, cotangent, chunk):
    one = jax.ShapeDtypeStruct((2 * tokens.shape[1], 2 * chunk + LANES), jnp.bfloat16)
    return pl.pallas_call(
        raw_kernel,
        out_shape=[one, one],
        in_specs=[VMEM, VMEM, HBM, HBM],
        out_specs=[VMEM] * 2,
        scratch_shapes=[pltpu.SemaphoreType.DMA((2, 2, 2))],
        compiler_params=pltpu.CompilerParams(vmem_limit_bytes=RAW_LIMIT * MIB),
        cost_estimate=SMALL,
        name="raw_rows",
    )(routes, gates, tokens, cotangent)


def pack_kernel(cap, routes, gates, tokens, cotangent, dropped, down, *refs):
    (next_near, next_far, near, local, pieces), (buffers, sems, piece_sems) = refs[:5], refs[5:]
    z, x, core, y = place()
    chunk = near.shape[1] // 2
    steps = [(dx, h) for dx in (0, 1) for h in (0, 1)]
    copies = []
    for i, (dx, h) in enumerate(steps):
        for j, source in enumerate((tokens, cotangent)):
            copies.append(
                pltpu.make_async_copy(
                    source.at[:, :, pl.ds(column_of(x, core, dx, h, chunk), chunk)],
                    buffers.at[i, j],
                    sems.at[i, j],
                )
            )
            copies[-1].start()
    piece_copies = pieces_to_send(dropped, down, pieces, piece_sems)
    for copy in piece_copies:
        copy.start()
    sets, placings, slot_gates = (y, 1 - y), [], []
    for s in sets:
        placing, gate = slots_of(
            rows_of(routes[s]), rows_of(gates[s].astype(jnp.float32)), (z, z ^ 1), cap
        )
        placings.append(placing)
        slot_gates.append(gate)
    next_near[:, 2 * chunk :] = gate_lanes([slot_gates[0][cap:]])
    local[:, 2 * chunk :] = gate_lanes([slot_gates[0][:cap], slot_gates[1][:cap]])
    for i, (dx, h) in enumerate(steps):
        copies[2 * i].wait()
        copies[2 * i + 1].wait()
        here = slice(h * chunk, (h + 1) * chunk)
        found = [
            jnp.dot(placing, buffers[i, j, s], preferred_element_type=jnp.float32)
            for s, placing in zip(sets, placings)
            for j in range(2)
        ]
        (next_near if dx == 0 else next_far)[:, here] = jnp.concatenate(
            [part[cap:] for part in found[:2]], axis=0
        ).astype(jnp.bfloat16)
        (local if dx == 0 else near)[:, here] = jnp.concatenate(
            [part[:cap] for part in found], axis=0
        ).astype(jnp.bfloat16)
    for copy in piece_copies:
        copy.wait()


def pack(routes, gates, tokens, cotangent, dropped, down, cap):
    def shape(rows, gated):
        return jax.ShapeDtypeStruct((rows, 2 * chunk + (LANES if gated else 0)), jnp.bfloat16)

    sets, rows = tokens.shape[:2]
    half, chunk = down.shape[1:]
    outs = [shape(2 * cap, True), shape(2 * cap, False), shape(4 * cap, False), shape(4 * cap, True)]
    return pl.pallas_call(
        functools.partial(pack_kernel, cap),
        out_shape=outs + [jax.ShapeDtypeStruct((SENT, half, chunk), down.dtype)],
        in_specs=[VMEM, VMEM, HBM, HBM, SMEM, HBM],
        out_specs=[VMEM] * 5,
        scratch_shapes=[
            pltpu.VMEM((4, 2, sets, rows, chunk), jnp.bfloat16),
            pltpu.SemaphoreType.DMA((4, 2)),
            pltpu.SemaphoreType.DMA((SENT,)),
        ],
        compiler_params=pltpu.CompilerParams(vmem_limit_bytes=PACK_LIMIT * MIB),
        cost_estimate=SMALL,
        name="pack_rows",
    )(routes, gates, tokens, cotangent, dropped, down)


def unpack_kernel(cap, top, gated, raw, mine, onward):
    z = lax.axis_index("expert")
    rows = raw.shape[0] // 2
    chunk = (raw.shape[1] - LANES) // 2
    notes = raw[:rows, 2 * chunk :].astype(jnp.float32)[:, :rows]
    route = [notes[k : k + 1].astype(jnp.int32) for k in range(top)]
    weight = [notes[top + k : top + k + 1] for k in range(top)]
    placing, gate = slots_of(route, weight, (z, z ^ 1), cap)
    if gated:
        mine[:, 2 * chunk :] = gate_lanes([gate[:cap]])
        onward[:, 2 * chunk :] = gate_lanes([gate[cap:]])
    for h in range(2):
        here = slice(h * chunk, (h + 1) * chunk)
        found = [
            jnp.dot(placing, raw[j * rows : (j + 1) * rows, here], preferred_element_type=jnp.float32)
            for j in range(2)
        ]
        mine[:, here] = jnp.concatenate([part[:cap] for part in found], axis=0).astype(jnp.bfloat16)
        onward[:, here] = jnp.concatenate([part[cap:] for part in found], axis=0).astype(jnp.bfloat16)


def unpack(raw, cap, top, gated):
    one = jax.ShapeDtypeStruct((2 * cap, raw.shape[1] - (0 if gated else LANES)), jnp.bfloat16)
    return pl.pallas_call(
        functools.partial(unpack_kernel, cap, top, gated),
        out_shape=[one, one],
        in_specs=[VMEM],
        out_specs=[VMEM] * 2,
        compiler_params=pltpu.CompilerParams(vmem_limit_bytes=16 * MIB),
        cost_estimate=SMALL,
        name="unpack_rows",
    )(raw)


def block_products(parts, weights, cap, put, width=256):
    chunk, inner = weights[0].shape
    left = jnp.concatenate([part[:, :chunk] for part in parts], axis=0)
    right = jnp.concatenate([part[:, chunk : 2 * chunk] for part in parts], axis=0)
    across = (((1,), (1,)), ((), ()))

    def along(columns, own, other):
        return jnp.dot(left, own[:, columns], preferred_element_type=jnp.float32) + jnp.dot(
            right, other[:, columns], preferred_element_type=jnp.float32
        )

    for at in range(0, inner, width):
        columns = slice(at, at + width)
        gate = along(columns, weights[0], weights[3])
        up = along(columns, weights[1], weights[4])
        product = lax.dot_general(
            left, weights[2][columns], across, preferred_element_type=jnp.float32
        ) + lax.dot_general(right, weights[5][columns], across, preferred_element_type=jnp.float32)
        for b in range(left.shape[0] // (2 * cap)):
            row = 2 * cap * b
            put(b, at, gate[row : row + cap], up[row : row + cap], product[row + cap : row + 2 * cap])


def gates_from(parts, cap, chunk):
    found = []
    for part in parts:
        lanes = part[:, 2 * chunk : 2 * chunk + LANES].astype(jnp.float32)
        found += [lanes[b : b + cap] for b in range(0, part.shape[0], 2 * cap)]
    return jnp.concatenate(found, axis=0)


def products_kernel(cap, width, n_sent, n_kept, *refs):
    n = n_sent + n_kept
    parts, weights, outs = refs[:n], refs[n : n + 6], refs[n + 6 :]
    chunk, inner = weights[0].shape
    half = outs[0].shape[0] // cap

    def put(b, at, *terms):
        rows = slice(b % half * cap, (b % half + 1) * cap)
        for i, term in enumerate(terms):
            outs[b // half][rows, i * inner + at : i * inner + at + width] = term

    if n_kept:
        outs[2][...] = gates_from(parts[n_sent:], cap, chunk)
    block_products(parts, weights, cap, put, width)


def products(sent, kept, weights, cap, width=256):
    chunk, inner = weights[0].shape
    half = sum(part.shape[0] for part in sent) // 2
    outs = [jax.ShapeDtypeStruct((half, 3 * inner), jnp.float32)]
    if kept:
        outs += [outs[0], jax.ShapeDtypeStruct((half, LANES), jnp.float32)]
    return pl.pallas_call(
        functools.partial(products_kernel, cap, width, len(sent), len(kept)),
        out_shape=outs,
        in_specs=[VMEM] * (len(sent) + len(kept) + 6),
        out_specs=[VMEM] * len(outs),
        compiler_params=pltpu.CompilerParams(vmem_limit_bytes=16 * MIB),
        cost_estimate=SMALL,
        name="partial_products",
    )(*sent, *kept, *weights)


def neuron_terms_of(gate, up, product, gates):
    return gate / (1.0 + jnp.exp(-gate)) * up * (gates * product)


def in_set_order(mine, other):
    y = lax.axis_index("tensor")
    return jnp.concatenate(
        [jnp.where(y == 0, mine, other), jnp.where(y == 0, other, mine)], axis=0
    )


def finish_kernel(cap, n, *refs):
    out = refs[-1]
    inner = out.shape[2]
    sums = [jnp.zeros((1, inner), jnp.float32)] * 2
    for g in range(n):
        kept, came, gates = refs[3 * g : 3 * g + 3]
        total = kept[...] + came[...]
        terms = neuron_terms_of(
            total[:, :inner], total[:, inner : 2 * inner], total[:, 2 * inner :], gates[:, :1]
        )
        for s in range(2):
            sums[s] = sums[s] + jnp.sum(terms[s * cap : (s + 1) * cap], axis=0, keepdims=True)
    out[:, 0, :] = in_set_order(*sums)


def finish(groups, cap):
    inner = groups[0][0].shape[1] // 3
    return pl.pallas_call(
        functools.partial(finish_kernel, cap, len(groups)),
        out_shape=jax.ShapeDtypeStruct((2, 1, inner), jnp.float32),
        in_specs=[VMEM] * (3 * len(groups)),
        out_specs=VMEM,
        compiler_params=pltpu.CompilerParams(vmem_limit_bytes=16 * MIB),
        cost_estimate=SMALL,
        name="neuron_sums",
    )(*[value for group in groups for value in group])


def last_kernel(cap, width, mine, other, *refs):
    weights, (came, before, out) = refs[:6], refs[6:]
    chunk, inner = weights[0].shape
    gates = gates_from([mine, other], cap, chunk)
    found = {}

    def put(b, at, *terms):
        rows = slice(b * cap, (b + 1) * cap)
        gate, up, product = (
            term + came[rows, i * inner + at : i * inner + at + width] for i, term in enumerate(terms)
        )
        found[b, at] = jnp.sum(
            neuron_terms_of(gate, up, product, gates[rows, :1]), axis=0, keepdims=True
        )

    block_products([mine, other], weights, cap, put, width)
    for at in range(0, inner, width):
        columns = slice(at, at + width)
        out[:, 0, columns] = before[:, 0, columns] + in_set_order(found[0, at], found[1, at])


def last(mine, other, weights, came, before, cap, width=256):
    chunk, inner = weights[0].shape
    return pl.pallas_call(
        functools.partial(last_kernel, cap, width),
        out_shape=jax.ShapeDtypeStruct((2, 1, inner), jnp.float32),
        in_specs=[VMEM] * 10,
        out_specs=VMEM,
        compiler_params=pltpu.CompilerParams(vmem_limit_bytes=16 * MIB),
        cost_estimate=SMALL,
        name="last_products",
    )(mine, other, *weights, came, before)


def kept_pieces(dropped):
    a, b, c = dropped[0, 0], dropped[0, 1], dropped[0, 2]
    low, high = jnp.minimum(jnp.minimum(a, b), c), jnp.maximum(jnp.maximum(a, b), c)
    middle = a + b + c - low - high

    def place_of(piece):
        block = piece // 2
        for one in (low, middle, high):
            block = block + (block >= one).astype(jnp.int32)
        return 2 * block + lax.rem(piece, 2)

    below = sum((one < NBLK // 2).astype(jnp.int32) for one in (a, b, c))
    return place_of, 2 * (NBLK // 2 - below)


def pieces_to_send(dropped, down, out, sems):
    y = lax.axis_index("tensor")
    place_of, low_pieces = kept_pieces(dropped)
    first = jnp.where(y == 0, KEEP, low_pieces)
    copies = []
    for i in range(out.shape[0]):
        piece = jnp.minimum(first + i, 2 * KEEP - 1)
        at = jnp.clip(place_of(piece) - NBLK * y, 0, NBLK - 1)
        copies.append(pltpu.make_async_copy(down.at[at], out.at[i], sems.at[i]))
    return copies


def keep_pieces_kernel(dropped, down, came, out, sems):
    y = lax.axis_index("tensor")
    place_of, low_pieces = kept_pieces(dropped)
    for i in range(KEEP):
        piece = KEEP * y + i
        is_low = (piece < low_pieces).astype(jnp.int32)
        near = jnp.where(y == 0, is_low, 1 - is_low)
        at = jnp.clip(place_of(piece) - NBLK * y, 0, NBLK - 1)
        far_at = jnp.clip(piece - jnp.where(y == 0, low_pieces, KEEP), 0, came.shape[0] - 1)

        @pl.when(near == 1)
        def _():
            pltpu.make_async_copy(down.at[at], out.at[i], sems.at[i]).start()

        @pl.when(near == 0)
        def _():
            pltpu.make_async_copy(came.at[far_at], out.at[i], sems.at[i]).start()

    for i in range(KEEP):
        pltpu.make_async_copy(down.at[0], out.at[i], sems.at[i]).wait()


def keep_pieces(dropped, down, came):
    return pl.pallas_call(
        keep_pieces_kernel,
        out_shape=jax.ShapeDtypeStruct((KEEP,) + down.shape[1:], down.dtype),
        in_specs=[SMEM, HBM, HBM],
        out_specs=VMEM,
        scratch_shapes=[pltpu.SemaphoreType.DMA((KEEP,))],
        compiler_params=pltpu.CompilerParams(vmem_limit_bytes=8 * MIB),
        cost_estimate=SMALL,
        name="kept_rows",
    )(dropped, down, came)


def paired_body(tokens, cotangent, route_gate, routes, gate_weight, up_weight, down_weight, dropped):
    experts = lax.axis_size("expert")
    groups = lax.axis_size("dp")
    cap = capacity_of(tokens.shape[1], routes.shape[2], experts)
    chunk = gate_weight.shape[1]

    def over_core(value):
        return lax.ppermute(value, "dp", [(d, d ^ 1) for d in range(groups)])

    def over_x(value):
        return lax.ppermute(value, "dp", [(d, d ^ 2) for d in range(groups)])

    def over_tensor(value):
        return lax.ppermute(value, "tensor", [(0, 1), (1, 0)])

    def over_expert(value, bit, dx):
        return lax.ppermute(
            value,
            ("expert", "dp"),
            [
                (e * groups + d, (e ^ bit) * groups + (d ^ (2 * dx)))
                for e in range(experts)
                for d in range(groups)
            ],
        )

    routes_in, gates_in = jnp.swapaxes(routes, 1, 2), jnp.swapaxes(route_gate, 1, 2)
    own = (gate_weight[0], up_weight[0], down_weight[0])
    down = own[2].reshape(NBLK, HALF, chunk)
    made = {}

    def get(name):
        if name not in made:
            made[name] = make(name[0], name[1:])
        return made[name]

    def after(value, name):
        others = tuple(get(one) for one in ORDER.get(name, ()))
        return lax.optimization_barrier((value,) + others)[0] if others else value

    def weights():
        return own + tuple(get("w" + str(i)) for i in range(3))

    def make(kind, rest):
        name = kind + rest
        if kind == "a":
            return raw_rows(routes_in, gates_in, tokens, cotangent, chunk)
        if kind == "m":
            return pack(after(routes_in, name), gates_in, tokens, cotangent, dropped, down, cap)
        if kind == "l":
            return get("m")[3]
        if kind == "n":
            return over_x(after(get("m")[2], name))
        if kind == "r":
            return over_expert(after(get("a")[int(rest)], name), 2, int(rest))
        if kind == "u":
            return unpack(get("r" + rest), cap, routes.shape[2], rest == "0")
        if kind == "c":
            k, dx = rest
            if k == "2":
                return get("u" + dx)[0]
            value = get("m")[int(dx)] if k == "1" else get("u" + dx)[1]
            return over_expert(after(value, name), 1, int(dx) if k == "1" else 0)
        if kind == "p":
            return over_tensor(after(get("c" + rest), name))
        if kind == "f":
            if rest == "0":
                return products([get("n")], [get("l")], weights(), cap)
            sent = [get("c" + rest + "1"), get("p" + rest + "1")]
            kept = [get("c" + rest + "0"), get("p" + rest + "0")] if rest == "1" else []
            return products(sent, kept, weights(), cap)
        if kind == "v":
            return last(get("c20"), get("p20"), weights(), get("x2"), get("t"), cap)
        if kind == "w":
            return over_core(after(own[int(rest)], name))
        if kind == "f":
            return products_of(rest)
        if kind == "s":
            return get("f" + rest)[0]
        if kind == "x":
            return over_x(after(get("s" + rest), name))
        if kind == "d":
            return over_tensor(after(get("m")[4], name))
        if kind == "k":
            return keep_pieces(dropped, down, get("d"))
        if kind == "t":
            return finish([(get("f" + g)[1], get("x" + g), get("f" + g)[2]) for g in "01"], cap)
        raise ValueError(name)

    totals = last(get("c30"), get("p30"), weights(), get("x3"), get("v"), cap)
    totals = totals + over_core(totals)
    saliency = jnp.abs(totals + over_x(totals))
    return saliency, get("k").reshape(1, KEEP * HALF, chunk)


def solution(mesh):
    sizes = mesh.shape
    paired = sizes["tensor"] == 2 and sizes["dp"] == 4 and sizes["expert"] == 4
    return jax.shard_map(
        paired_body if paired else general_body,
        mesh=mesh,
        in_specs=(
            P(None, ("expert", "dp"), None),
            P(None, ("expert", "dp"), None),
            P(None, ("expert", "dp"), None),
            P(None, ("expert", "dp"), None),
            P("expert", "dp", "tensor"),
            P("expert", "dp", "tensor"),
            P("expert", "tensor", "dp"),
            P("expert", None),
        ),
        out_specs=(P(None, "expert", "tensor"), P("expert", "tensor", "dp")),
        check_vma=False,
    )
```

```python
import functools

import jax
import jax.numpy as jnp
from jax import lax
from jax.experimental import pallas as pl
from jax.experimental.pallas import tpu as pltpu
from jax.sharding import PartitionSpec as P

BLOCK = 128
NBLK = 8
KEEP = 5
LANES = 128
HALF = 64
MIB = 1 << 20
RAW_LIMIT = 24
PACK_LIMIT = 24
SENT = 3
ORDER = {
    "c10": ("r1",),
    "c30": ("p21", "x0",),
    "c31": ("p11",),
    "m": ("a",),
    "n": ("w0", "w1", "w2",),
    "p10": ("d",),
    "p30": ("p20", "s2", "t",),
    "x0": ("k",),
    "x3": ("x2",),
}
SMALL = pl.CostEstimate(flops=0, bytes_accessed=0, transcendentals=0)


def capacity_of(tok_rows, top_count, experts):
    return min(tok_rows, max(2, 3 * tok_rows * top_count // (2 * experts)))


def neuron_terms(x_recv, grad_recv, gate_recv, gate_full, up_full, down_full):
    gate_act = jnp.einsum("pscd,df->pscf", x_recv, gate_full, preferred_element_type=jnp.float32)
    up_act = jnp.einsum("pscd,df->pscf", x_recv, up_full, preferred_element_type=jnp.float32)
    hidden = jax.nn.silu(gate_act) * up_act
    product = jnp.einsum("pscd,fd->pscf", grad_recv, down_full, preferred_element_type=jnp.float32)
    hidden_grad = gate_recv.astype(jnp.float32)[..., None] * product
    return jnp.sum(hidden * hidden_grad, axis=(0, 2))


def kept_blocks(dropped):
    blocks = jnp.arange(NBLK, dtype=jnp.int32)
    kept_flag = jnp.all(dropped[0][:, None] != blocks[None, :], axis=0)
    ranking = jnp.cumsum(kept_flag.astype(jnp.int32)) - 1
    ranks = jnp.arange(KEEP, dtype=jnp.int32)
    chosen = kept_flag[None, :] & (ranking[None, :] == ranks[:, None])
    return jnp.sum(jnp.where(chosen, blocks[None, :], 0), axis=1), kept_flag


def general_body(tokens, cotangent, route_gate, routes, gate_weight, up_weight, down_weight, dropped):
    experts = lax.axis_size("expert")
    tensor_count = lax.axis_size("tensor")
    tensor_pos = lax.axis_index("tensor")
    tok_rows = tokens.shape[1]
    capacity = capacity_of(tok_rows, routes.shape[2], experts)
    expert_ids = jnp.arange(experts, dtype=jnp.int32)
    matched = routes[:, :, :, None] == expert_ids
    chosen = jnp.any(matched, axis=2).astype(jnp.float32)
    weight_sum = jnp.sum(
        jnp.where(matched, route_gate.astype(jnp.float32)[:, :, :, None], 0.0), axis=2
    )
    earlier = jnp.cumsum(chosen, axis=1) - chosen
    placing = chosen[..., None] * (earlier[..., None] == jnp.arange(capacity, dtype=jnp.float32))
    slot_gate = jnp.einsum("stec,ste->esc", placing, weight_sum, precision=lax.Precision.HIGHEST)
    gate_slots = slot_gate.astype(jnp.bfloat16)
    placing_half = placing.astype(jnp.bfloat16)
    gate_full = lax.all_gather(gate_weight, "dp", axis=1, tiled=True)[0]
    up_full = lax.all_gather(up_weight, "dp", axis=1, tiled=True)[0]
    down_full = lax.all_gather(down_weight, "dp", axis=2, tiled=True)[0]
    x_slots = jnp.einsum(
        "stec,std->escd", placing_half, tokens, preferred_element_type=jnp.float32
    ).astype(jnp.bfloat16)
    grad_slots = jnp.einsum(
        "stec,std->escd", placing_half, cotangent, preferred_element_type=jnp.float32
    ).astype(jnp.bfloat16)
    partial_terms = neuron_terms(
        lax.all_to_all(x_slots, "expert", split_axis=0, concat_axis=0, tiled=True),
        lax.all_to_all(grad_slots, "expert", split_axis=0, concat_axis=0, tiled=True),
        lax.all_to_all(gate_slots, "expert", split_axis=0, concat_axis=0, tiled=True),
        gate_full,
        up_full,
        down_full,
    )
    totals = lax.psum(partial_terms, "dp")
    saliency = jnp.abs(totals)[:, None, :]
    rows_out = KEEP * BLOCK // tensor_count
    whole_rows = lax.all_gather(down_weight, "tensor", axis=1, tiled=True)[0]
    target_rows = tensor_pos * rows_out + jnp.arange(rows_out, dtype=jnp.int32)
    source_rows = kept_blocks(dropped)[0][target_rows // BLOCK] * BLOCK + target_rows % BLOCK
    compact_down = jnp.take(whole_rows, source_rows, axis=0)[None]
    return (saliency, compact_down)


VMEM = pl.BlockSpec(memory_space=pltpu.VMEM)
HBM = pl.BlockSpec(memory_space=pltpu.HBM)
SMEM = pl.BlockSpec(memory_space=pltpu.SMEM)


def place():
    dp = lax.axis_index("dp")
    return lax.axis_index("expert"), dp // 2, lax.rem(dp, 2), lax.axis_index("tensor")


def slots_of(route, weight, experts, cap):
    rows = route[0].shape[1]
    count = len(experts) * cap
    line = lax.broadcasted_iota(jnp.int32, (count, rows), 0)
    expert = jnp.full((count, rows), experts[0], jnp.int32)
    slot = line
    for i, other in enumerate(experts[1:], 1):
        expert = jnp.where(line >= i * cap, other, expert)
        slot = jnp.where(line >= i * cap, line - i * cap, slot)
    earlier = (
        lax.broadcasted_iota(jnp.int32, (rows, rows), 0)
        < lax.broadcasted_iota(jnp.int32, (rows, rows), 1)
    ).astype(jnp.bfloat16)
    match = jnp.zeros((count, rows), jnp.float32)
    named = jnp.zeros((count, rows), jnp.float32)
    for r, w in zip(route, weight):
        same = r == expert
        match = match + jnp.where(same, 1.0, 0.0)
        named = named + jnp.where(same, w, 0.0)
    rank = jnp.dot(match.astype(jnp.bfloat16), earlier, preferred_element_type=jnp.float32)
    placing = jnp.where(rank == slot.astype(jnp.float32), match, 0.0)
    return placing.astype(jnp.bfloat16), jnp.sum(placing * named, axis=1, keepdims=True)


def gate_lanes(columns):
    blocks = []
    for column in columns:
        blocks += [jnp.broadcast_to(column, (column.shape[0], LANES)), jnp.zeros((column.shape[0], LANES), jnp.float32)]
    return jnp.concatenate(blocks, axis=0).astype(jnp.bfloat16)


def rows_of(value):
    return [value[k : k + 1] for k in range(value.shape[0])]


def column_of(x, core, dx, h, chunk):
    half = x if dx == 0 else 1 - x
    return pl.multiple_of((2 * half + (core if h == 0 else 1 - core)) * chunk, LANES)


def raw_kernel(routes, gates, tokens, cotangent, near, far, sems):
    _, x, core, y = place()
    rows = tokens.shape[1]
    chunk = (far.shape[1] - LANES) // 2
    copies = []
    for dx, out in ((1, far), (0, near)):
        for h in range(2):
            for j, source in enumerate((tokens, cotangent)):
                copies.append(
                    pltpu.make_async_copy(
                        source.at[y, :, pl.ds(column_of(x, core, dx, h, chunk), chunk)],
                        out.at[pl.ds(j * rows, rows), pl.ds(h * chunk, chunk)],
                        sems.at[dx, h, j],
                    )
                )
                copies[-1].start()
    line = lax.broadcasted_iota(jnp.int32, (2 * rows, rows), 0)
    notes = jnp.zeros((2 * rows, rows), jnp.float32)
    for i, row in enumerate(rows_of(routes[y].astype(jnp.float32)) + rows_of(gates[y].astype(jnp.float32))):
        notes = jnp.where(line == i, row, notes)
    notes = notes.astype(jnp.bfloat16)
    for out in (far, near):
        out[:, 2 * chunk :] = jnp.zeros((2 * rows, LANES), jnp.bfloat16)
        out[:, 2 * chunk : 2 * chunk + rows] = notes
    for copy in copies:
        copy.wait()


def raw_rows(routes, gates, tokens, cotangent, chunk):
    one = jax.ShapeDtypeStruct((2 * tokens.shape[1], 2 * chunk + LANES), jnp.bfloat16)
    return pl.pallas_call(
        raw_kernel,
        out_shape=[one, one],
        in_specs=[VMEM, VMEM, HBM, HBM],
        out_specs=[VMEM] * 2,
        scratch_shapes=[pltpu.SemaphoreType.DMA((2, 2, 2))],
        compiler_params=pltpu.CompilerParams(vmem_limit_bytes=RAW_LIMIT * MIB),
        cost_estimate=SMALL,
        name="raw_rows",
    )(routes, gates, tokens, cotangent)


def pack_kernel(cap, routes, gates, tokens, cotangent, dropped, down, *refs):
    (next_near, next_far, near, local, pieces), (buffers, sems, piece_sems) = refs[:5], refs[5:]
    z, x, core, y = place()
    chunk = near.shape[1] // 2
    steps = [(dx, h) for dx in (0, 1) for h in (0, 1)]
    copies = []
    for i, (dx, h) in enumerate(steps):
        for j, source in enumerate((tokens, cotangent)):
            copies.append(
                pltpu.make_async_copy(
                    source.at[:, :, pl.ds(column_of(x, core, dx, h, chunk), chunk)],
                    buffers.at[i, j],
                    sems.at[i, j],
                )
            )
            copies[-1].start()
    piece_copies = pieces_to_send(dropped, down, pieces, piece_sems)
    for copy in piece_copies:
        copy.start()
    sets, placings, slot_gates = (y, 1 - y), [], []
    for s in sets:
        placing, gate = slots_of(
            rows_of(routes[s]), rows_of(gates[s].astype(jnp.float32)), (z, z ^ 1), cap
        )
        placings.append(placing)
        slot_gates.append(gate)
    next_near[:, 2 * chunk :] = gate_lanes([slot_gates[0][cap:]])
    local[:, 2 * chunk :] = gate_lanes([slot_gates[0][:cap], slot_gates[1][:cap]])
    for i, (dx, h) in enumerate(steps):
        copies[2 * i].wait()
        copies[2 * i + 1].wait()
        here = slice(h * chunk, (h + 1) * chunk)
        found = [
            jnp.dot(placing, buffers[i, j, s], preferred_element_type=jnp.float32)
            for s, placing in zip(sets, placings)
            for j in range(2)
        ]
        (next_near if dx == 0 else next_far)[:, here] = jnp.concatenate(
            [part[cap:] for part in found[:2]], axis=0
        ).astype(jnp.bfloat16)
        (local if dx == 0 else near)[:, here] = jnp.concatenate(
            [part[:cap] for part in found], axis=0
        ).astype(jnp.bfloat16)
    for copy in piece_copies:
        copy.wait()


def pack(routes, gates, tokens, cotangent, dropped, down, cap):
    def shape(rows, gated):
        return jax.ShapeDtypeStruct((rows, 2 * chunk + (LANES if gated else 0)), jnp.bfloat16)

    sets, rows = tokens.shape[:2]
    half, chunk = down.shape[1:]
    outs = [shape(2 * cap, True), shape(2 * cap, False), shape(4 * cap, False), shape(4 * cap, True)]
    return pl.pallas_call(
        functools.partial(pack_kernel, cap),
        out_shape=outs + [jax.ShapeDtypeStruct((SENT, half, chunk), down.dtype)],
        in_specs=[VMEM, VMEM, HBM, HBM, SMEM, HBM],
        out_specs=[VMEM] * 5,
        scratch_shapes=[
            pltpu.VMEM((4, 2, sets, rows, chunk), jnp.bfloat16),
            pltpu.SemaphoreType.DMA((4, 2)),
            pltpu.SemaphoreType.DMA((SENT,)),
        ],
        compiler_params=pltpu.CompilerParams(vmem_limit_bytes=PACK_LIMIT * MIB),
        cost_estimate=SMALL,
        name="pack_rows",
    )(routes, gates, tokens, cotangent, dropped, down)


def unpack_kernel(cap, top, gated, raw, mine, onward):
    z = lax.axis_index("expert")
    rows = raw.shape[0] // 2
    chunk = (raw.shape[1] - LANES) // 2
    notes = raw[:rows, 2 * chunk :].astype(jnp.float32)[:, :rows]
    route = [notes[k : k + 1].astype(jnp.int32) for k in range(top)]
    weight = [notes[top + k : top + k + 1] for k in range(top)]
    placing, gate = slots_of(route, weight, (z, z ^ 1), cap)
    if gated:
        mine[:, 2 * chunk :] = gate_lanes([gate[:cap]])
        onward[:, 2 * chunk :] = gate_lanes([gate[cap:]])
    for h in range(2):
        here = slice(h * chunk, (h + 1) * chunk)
        found = [
            jnp.dot(placing, raw[j * rows : (j + 1) * rows, here], preferred_element_type=jnp.float32)
            for j in range(2)
        ]
        mine[:, here] = jnp.concatenate([part[:cap] for part in found], axis=0).astype(jnp.bfloat16)
        onward[:, here] = jnp.concatenate([part[cap:] for part in found], axis=0).astype(jnp.bfloat16)


def unpack(raw, cap, top, gated):
    one = jax.ShapeDtypeStruct((2 * cap, raw.shape[1] - (0 if gated else LANES)), jnp.bfloat16)
    return pl.pallas_call(
        functools.partial(unpack_kernel, cap, top, gated),
        out_shape=[one, one],
        in_specs=[VMEM],
        out_specs=[VMEM] * 2,
        compiler_params=pltpu.CompilerParams(vmem_limit_bytes=16 * MIB),
        cost_estimate=SMALL,
        name="unpack_rows",
    )(raw)


def block_products(parts, weights, cap, put, width=256):
    chunk, inner = weights[0].shape
    left = jnp.concatenate([part[:, :chunk] for part in parts], axis=0)
    right = jnp.concatenate([part[:, chunk : 2 * chunk] for part in parts], axis=0)
    across = (((1,), (1,)), ((), ()))

    def along(columns, own, other):
        return jnp.dot(left, own[:, columns], preferred_element_type=jnp.float32) + jnp.dot(
            right, other[:, columns], preferred_element_type=jnp.float32
        )

    for at in range(0, inner, width):
        columns = slice(at, at + width)
        gate = along(columns, weights[0], weights[3])
        up = along(columns, weights[1], weights[4])
        product = lax.dot_general(
            left, weights[2][columns], across, preferred_element_type=jnp.float32
        ) + lax.dot_general(right, weights[5][columns], across, preferred_element_type=jnp.float32)
        for b in range(left.shape[0] // (2 * cap)):
            row = 2 * cap * b
            put(b, at, gate[row : row + cap], up[row : row + cap], product[row + cap : row + 2 * cap])


def gates_from(parts, cap, chunk):
    found = []
    for part in parts:
        lanes = part[:, 2 * chunk : 2 * chunk + LANES].astype(jnp.float32)
        found += [lanes[b : b + cap] for b in range(0, part.shape[0], 2 * cap)]
    return jnp.concatenate(found, axis=0)


def products_kernel(cap, width, n_sent, n_kept, *refs):
    n = n_sent + n_kept
    parts, weights, outs = refs[:n], refs[n : n + 6], refs[n + 6 :]
    chunk, inner = weights[0].shape
    half = outs[0].shape[0] // cap

    def put(b, at, *terms):
        rows = slice(b % half * cap, (b % half + 1) * cap)
        for i, term in enumerate(terms):
            outs[b // half][rows, i * inner + at : i * inner + at + width] = term

    if n_kept:
        outs[2][...] = gates_from(parts[n_sent:], cap, chunk)
    block_products(parts, weights, cap, put, width)


def products(sent, kept, weights, cap, width=256):
    chunk, inner = weights[0].shape
    half = sum(part.shape[0] for part in sent) // 2
    outs = [jax.ShapeDtypeStruct((half, 3 * inner), jnp.float32)]
    if kept:
        outs += [outs[0], jax.ShapeDtypeStruct((half, LANES), jnp.float32)]
    return pl.pallas_call(
        functools.partial(products_kernel, cap, width, len(sent), len(kept)),
        out_shape=outs,
        in_specs=[VMEM] * (len(sent) + len(kept) + 6),
        out_specs=[VMEM] * len(outs),
        compiler_params=pltpu.CompilerParams(vmem_limit_bytes=16 * MIB),
        cost_estimate=SMALL,
        name="partial_products",
    )(*sent, *kept, *weights)


def neuron_terms_of(gate, up, product, gates):
    return gate / (1.0 + jnp.exp(-gate)) * up * (gates * product)


def in_set_order(mine, other):
    y = lax.axis_index("tensor")
    return jnp.concatenate(
        [jnp.where(y == 0, mine, other), jnp.where(y == 0, other, mine)], axis=0
    )


def finish_kernel(cap, n, *refs):
    out = refs[-1]
    inner = out.shape[2]
    sums = [jnp.zeros((1, inner), jnp.float32)] * 2
    for g in range(n):
        kept, came, gates = refs[3 * g : 3 * g + 3]
        total = kept[...] + came[...]
        terms = neuron_terms_of(
            total[:, :inner], total[:, inner : 2 * inner], total[:, 2 * inner :], gates[:, :1]
        )
        for s in range(2):
            sums[s] = sums[s] + jnp.sum(terms[s * cap : (s + 1) * cap], axis=0, keepdims=True)
    out[:, 0, :] = in_set_order(*sums)


def finish(groups, cap):
    inner = groups[0][0].shape[1] // 3
    return pl.pallas_call(
        functools.partial(finish_kernel, cap, len(groups)),
        out_shape=jax.ShapeDtypeStruct((2, 1, inner), jnp.float32),
        in_specs=[VMEM] * (3 * len(groups)),
        out_specs=VMEM,
        compiler_params=pltpu.CompilerParams(vmem_limit_bytes=16 * MIB),
        cost_estimate=SMALL,
        name="neuron_sums",
    )(*[value for group in groups for value in group])


def last_kernel(cap, width, mine, other, *refs):
    weights, (came, before, out) = refs[:6], refs[6:]
    chunk, inner = weights[0].shape
    gates = gates_from([mine, other], cap, chunk)
    found = {}

    def put(b, at, *terms):
        rows = slice(b * cap, (b + 1) * cap)
        gate, up, product = (
            term + came[rows, i * inner + at : i * inner + at + width] for i, term in enumerate(terms)
        )
        found[b, at] = jnp.sum(
            neuron_terms_of(gate, up, product, gates[rows, :1]), axis=0, keepdims=True
        )

    block_products([mine, other], weights, cap, put, width)
    for at in range(0, inner, width):
        columns = slice(at, at + width)
        out[:, 0, columns] = before[:, 0, columns] + in_set_order(found[0, at], found[1, at])


def last(mine, other, weights, came, before, cap, width=256):
    chunk, inner = weights[0].shape
    return pl.pallas_call(
        functools.partial(last_kernel, cap, width),
        out_shape=jax.ShapeDtypeStruct((2, 1, inner), jnp.float32),
        in_specs=[VMEM] * 10,
        out_specs=VMEM,
        compiler_params=pltpu.CompilerParams(vmem_limit_bytes=16 * MIB),
        cost_estimate=SMALL,
        name="last_products",
    )(mine, other, *weights, came, before)


def kept_pieces(dropped):
    a, b, c = dropped[0, 0], dropped[0, 1], dropped[0, 2]
    low, high = jnp.minimum(jnp.minimum(a, b), c), jnp.maximum(jnp.maximum(a, b), c)
    middle = a + b + c - low - high

    def place_of(piece):
        block = piece // 2
        for one in (low, middle, high):
            block = block + (block >= one).astype(jnp.int32)
        return 2 * block + lax.rem(piece, 2)

    below = sum((one < NBLK // 2).astype(jnp.int32) for one in (a, b, c))
    return place_of, 2 * (NBLK // 2 - below)


def pieces_to_send(dropped, down, out, sems):
    y = lax.axis_index("tensor")
    place_of, low_pieces = kept_pieces(dropped)
    first = jnp.where(y == 0, KEEP, low_pieces)
    copies = []
    for i in range(out.shape[0]):
        piece = jnp.minimum(first + i, 2 * KEEP - 1)
        at = jnp.clip(place_of(piece) - NBLK * y, 0, NBLK - 1)
        copies.append(pltpu.make_async_copy(down.at[at], out.at[i], sems.at[i]))
    return copies


def keep_pieces_kernel(dropped, down, came, out, sems):
    y = lax.axis_index("tensor")
    place_of, low_pieces = kept_pieces(dropped)
    for i in range(KEEP):
        piece = KEEP * y + i
        is_low = (piece < low_pieces).astype(jnp.int32)
        near = jnp.where(y == 0, is_low, 1 - is_low)
        at = jnp.clip(place_of(piece) - NBLK * y, 0, NBLK - 1)
        far_at = jnp.clip(piece - jnp.where(y == 0, low_pieces, KEEP), 0, came.shape[0] - 1)

        @pl.when(near == 1)
        def _():
            pltpu.make_async_copy(down.at[at], out.at[i], sems.at[i]).start()

        @pl.when(near == 0)
        def _():
            pltpu.make_async_copy(came.at[far_at], out.at[i], sems.at[i]).start()

    for i in range(KEEP):
        pltpu.make_async_copy(down.at[0], out.at[i], sems.at[i]).wait()


def keep_pieces(dropped, down, came):
    return pl.pallas_call(
        keep_pieces_kernel,
        out_shape=jax.ShapeDtypeStruct((KEEP,) + down.shape[1:], down.dtype),
        in_specs=[SMEM, HBM, HBM],
        out_specs=VMEM,
        scratch_shapes=[pltpu.SemaphoreType.DMA((KEEP,))],
        compiler_params=pltpu.CompilerParams(vmem_limit_bytes=8 * MIB),
        cost_estimate=SMALL,
        name="kept_rows",
    )(dropped, down, came)


def paired_body(tokens, cotangent, route_gate, routes, gate_weight, up_weight, down_weight, dropped):
    experts = lax.axis_size("expert")
    groups = lax.axis_size("dp")
    cap = capacity_of(tokens.shape[1], routes.shape[2], experts)
    chunk = gate_weight.shape[1]

    def over_core(value):
        return lax.ppermute(value, "dp", [(d, d ^ 1) for d in range(groups)])

    def over_x(value):
        return lax.ppermute(value, "dp", [(d, d ^ 2) for d in range(groups)])

    def over_tensor(value):
        return lax.ppermute(value, "tensor", [(0, 1), (1, 0)])

    def over_expert(value, bit, dx):
        return lax.ppermute(
            value,
            ("expert", "dp"),
            [
                (e * groups + d, (e ^ bit) * groups + (d ^ (2 * dx)))
                for e in range(experts)
                for d in range(groups)
            ],
        )

    routes_in, gates_in = jnp.swapaxes(routes, 1, 2), jnp.swapaxes(route_gate, 1, 2)
    own = (gate_weight[0], up_weight[0], down_weight[0])
    down = own[2].reshape(NBLK, HALF, chunk)
    made = {}

    def get(name):
        if name not in made:
            made[name] = make(name[0], name[1:])
        return made[name]

    def after(value, name):
        others = tuple(get(one) for one in ORDER.get(name, ()))
        return lax.optimization_barrier((value,) + others)[0] if others else value

    def weights():
        return own + tuple(get("w" + str(i)) for i in range(3))

    def make(kind, rest):
        name = kind + rest
        if kind == "a":
            return raw_rows(routes_in, gates_in, tokens, cotangent, chunk)
        if kind == "m":
            return pack(after(routes_in, name), gates_in, tokens, cotangent, dropped, down, cap)
        if kind == "l":
            return get("m")[3]
        if kind == "n":
            return over_x(after(get("m")[2], name))
        if kind == "r":
            return over_expert(after(get("a")[int(rest)], name), 2, int(rest))
        if kind == "u":
            return unpack(get("r" + rest), cap, routes.shape[2], rest == "0")
        if kind == "c":
            k, dx = rest
            if k == "2":
                return get("u" + dx)[0]
            value = get("m")[int(dx)] if k == "1" else get("u" + dx)[1]
            return over_expert(after(value, name), 1, int(dx) if k == "1" else 0)
        if kind == "p":
            return over_tensor(after(get("c" + rest), name))
        if kind == "f":
            if rest == "0":
                return products([get("n")], [get("l")], weights(), cap)
            sent = [get("c" + rest + "1"), get("p" + rest + "1")]
            kept = [get("c" + rest + "0"), get("p" + rest + "0")] if rest == "1" else []
            return products(sent, kept, weights(), cap)
        if kind == "v":
            return last(get("c20"), get("p20"), weights(), get("x2"), get("t"), cap)
        if kind == "w":
            return over_core(after(own[int(rest)], name))
        if kind == "f":
            return products_of(rest)
        if kind == "s":
            return get("f" + rest)[0]
        if kind == "x":
            return over_x(after(get("s" + rest), name))
        if kind == "d":
            return over_tensor(after(get("m")[4], name))
        if kind == "k":
            return keep_pieces(dropped, down, get("d"))
        if kind == "t":
            return finish([(get("f" + g)[1], get("x" + g), get("f" + g)[2]) for g in "01"], cap)
        raise ValueError(name)

    totals = last(get("c30"), get("p30"), weights(), get("x3"), get("v"), cap)
    totals = totals + over_core(totals)
    saliency = jnp.abs(totals + over_x(totals))
    return saliency, get("k").reshape(1, KEEP * HALF, chunk)


def solution(mesh):
    sizes = mesh.shape
    paired = sizes["tensor"] == 2 and sizes["dp"] == 4 and sizes["expert"] == 4
    return jax.shard_map(
        paired_body if paired else general_body,
        mesh=mesh,
        in_specs=(
            P(None, ("expert", "dp"), None),
            P(None, ("expert", "dp"), None),
            P(None, ("expert", "dp"), None),
            P(None, ("expert", "dp"), None),
            P("expert", "dp", "tensor"),
            P("expert", "dp", "tensor"),
            P("expert", "tensor", "dp"),
            P("expert", None),
        ),
        out_specs=(P(None, "expert", "tensor"), P("expert", "tensor", "dp")),
        check_vma=False,
    )
```
